32 devices in a mesh: sky: 16 (over z, y, core), loop: 2 (over x).
Axes of the slice: x: 2, y: 2, z: 4, core: 2. Of those that a mesh axis runs over, the one named last changes fastest.
Arguments:
- queries: bfloat16 [24576, 256], P(('sky', 'loop')), may hold values from -1 to 1
- keys: bfloat16 [24576, 256], P(('sky', 'loop')), may hold values from -1 to 1
- partner_owner: int32 [24576, 4], P(('sky', 'loop')), may hold values from 0 to 15, as said below
- partner_row: int32 [24576, 4], P(('sky', 'loop')), may hold values from 0 to 767
- partner_count: int32 [24576], P(('sky', 'loop')), may hold values from 1 to 4, as said below
Outputs:
- loss: float32 [24576], P(('sky', 'loop'))
- grad_queries: float32 [24576, 256], P(('sky', 'loop'))
- grad_keys: float32 [24576, 256], P(('sky', 'loop'))
The draws below stay inside these ranges and needn't reach their ends.
Inputs may be any that keep to these rules, and one draw needn't show every extreme that they name: `partner_owner`: each row names 4 different sky indices, never its own device's sky index; among the rows of one device no index is named more than 384 times, and on every device some index is named exactly 384 times. `partner_count`: some anchor has 4 live partners and some has one.
All inputs are finite; a program needn't handle non-finite values.
Results may differ from the reference program's by a relative error of at most 0.004.
Values may be sent and summed in bfloat16 or wider, within the bound.
No kernel may reach another device: no remote copies, remote signals or barrier semaphores. Data moves between devices by JAX's collectives and lax.ppermute only.
A program may use at most 64 MiB of HBM per device.

```python
import jax
import jax.numpy as jnp
from jax import lax

D = 256
ANCHORS = 768
PARTNERS = 4
BUCKET = 384
GROUP = 1536
ROWS = 24576
N_LOOP = 2


def draw_codes(key):
    devices = ROWS // ANCHORS
    subkeys = jax.random.split(jax.random.fold_in(key, 31), devices)
    return jax.vmap(lambda subkey: jax.random.permutation(subkey, ANCHORS))(subkeys).astype(jnp.int32)


def draw_routes(key):
    devices = ROWS // ANCHORS
    sky_count = ROWS // GROUP
    others = sky_count - 1
    couples = (sky_count - 2) // 2
    codes = draw_codes(key)
    device_ids = jnp.arange(devices, dtype=jnp.int32)
    sky_of = device_ids // N_LOOP
    loop_of = device_ids % N_LOOP
    hot = jax.random.randint(jax.random.fold_in(key, 32), (), 0, sky_count, dtype=jnp.int32)
    rank_keys = jax.random.split(jax.random.fold_in(key, 33), devices)
    ranks = jax.vmap(lambda subkey: jax.random.permutation(subkey, others))(rank_keys).astype(jnp.int32)
    spare = jax.random.randint(jax.random.fold_in(key, 34), (devices,), 1, sky_count, dtype=jnp.int32)
    hot_offset = jnp.where(sky_of == hot, spare, (hot - sky_of) % sky_count)
    offsets = jnp.arange(others, dtype=jnp.int32)[None, :] + 1
    ranks = jnp.where(offsets == hot_offset[:, None], -1, ranks)
    order = (jnp.argsort(ranks, axis=1, stable=True) + 1).astype(jnp.int32)
    split_at = jax.random.randint(jax.random.fold_in(key, 35), (devices, couples), 0, BUCKET + 1, dtype=jnp.int32)
    paired = jnp.stack([split_at, BUCKET - split_at], axis=2).reshape(devices, 2 * couples)
    counts = jnp.concatenate([jnp.full((devices, 1), BUCKET, jnp.int32), paired], axis=1)
    ends = jnp.cumsum(counts, axis=1)
    position = jnp.arange(ANCHORS * PARTNERS, dtype=jnp.int32)
    which = jnp.sum((position[None, :, None] >= ends[:, None, :]).astype(jnp.int32), axis=2)
    offset = jnp.take_along_axis(order, which, axis=1)
    owner_flat = (sky_of[:, None] + offset) % sky_count
    arranged = owner_flat.reshape(devices, PARTNERS, ANCHORS).transpose(0, 2, 1)
    shuffle_keys = jax.random.split(jax.random.fold_in(key, 36), devices)
    shuffle = jax.vmap(lambda subkey: jax.random.permutation(subkey, ANCHORS))(shuffle_keys).astype(jnp.int32)
    owner = jnp.take_along_axis(arranged, shuffle[:, :, None], axis=1)
    inverse_codes = jax.vmap(lambda code: jnp.zeros((ANCHORS,), jnp.int32).at[code].set(jnp.arange(ANCHORS, dtype=jnp.int32)))(codes)
    partner_device = owner * N_LOOP + loop_of[:, None, None]
    own_code = jnp.broadcast_to(codes[:, :, None], owner.shape)
    row = inverse_codes[partner_device, own_code]
    return (owner.reshape(ROWS, PARTNERS).astype(jnp.int32), row.reshape(ROWS, PARTNERS).astype(jnp.int32))


def draw_side(key, salt):
    devices = ROWS // ANCHORS
    codes = draw_codes(key)
    loop_of = jnp.arange(devices, dtype=jnp.int32) % N_LOOP
    code_global = (loop_of[:, None] * ANCHORS + codes).reshape(ROWS)
    latent = jax.random.truncated_normal(jax.random.fold_in(key, 41), -3.0, 3.0, (N_LOOP * ANCHORS, D), jnp.float32)
    own_part = jax.random.truncated_normal(jax.random.fold_in(key, salt), -3.0, 3.0, (ROWS, D), jnp.float32)
    value = jnp.take(latent, code_global, axis=0) + 0.6 * own_part
    return jnp.clip(value / jnp.sqrt(jnp.float32(D)), -1.0, 1.0)


def draw_queries(key, part):
    return draw_side(key, 21).astype(jnp.bfloat16)


def draw_keys(key, part):
    return draw_side(key, 22).astype(jnp.bfloat16)


def draw_partner_owner(key, part):
    return draw_routes(key)[0]


def draw_partner_row(key, part):
    return draw_routes(key)[1]


def draw_partner_count(key, part):
    counts = jax.random.randint(jax.random.fold_in(key, 5), (ROWS,), 1, PARTNERS + 1, dtype=jnp.int32)
    return counts.at[0].set(PARTNERS).at[1].set(1)


def setup_inputs(seed: int = 0) -> dict:
    splits = jax.random.split(jax.random.key(seed), 6)
    return {
        "queries": draw_queries(jax.random.fold_in(splits[5], 71), 0),
        "keys": draw_keys(jax.random.fold_in(splits[5], 71), 0),
        "partner_owner": draw_partner_owner(jax.random.fold_in(splits[5], 71), 0),
        "partner_row": draw_partner_row(jax.random.fold_in(splits[5], 71), 0),
        "partner_count": draw_partner_count(jax.random.fold_in(splits[5], 71), 0),
    }


SCALE = 10.0
EPS = 1e-06

def unit_rows(rows):
    wide = rows.astype(jnp.float32)
    norms = jnp.sqrt(lax.optimization_barrier(jnp.sum(wide * wide, axis=-1, keepdims=True)) + EPS)
    return (wide / norms, norms)

def back_unit(unit, norms, grad):
    return (grad - unit * lax.optimization_barrier(jnp.sum(unit * grad, axis=-1, keepdims=True))) / norms

def reference(queries, keys, partner_owner, partner_row, partner_count):
    unit_q, norm_q = unit_rows(queries)
    unit_k, norm_k = unit_rows(keys)
    query_rows = unit_q.astype(jnp.bfloat16)
    key_rows = unit_k.astype(jnp.bfloat16)
    rows_all = jnp.arange(ROWS, dtype=jnp.int32)
    loop_place = rows_all // ANCHORS % N_LOOP
    partner_index = ((partner_owner * N_LOOP + loop_place[:, None]) * ANCHORS + partner_row).astype(jnp.int32)
    valid = jnp.arange(PARTNERS, dtype=jnp.int32)[None, :] < partner_count[:, None]
    inverse = 1.0 / (1.0 + partner_count.astype(jnp.float32))
    group_count = ROWS // GROUP

    def one_group(carry, index):
        begin = (index * GROUP).astype(jnp.int32)
        q_block = lax.dynamic_slice_in_dim(query_rows, begin, GROUP)
        k_block = lax.dynamic_slice_in_dim(key_rows, begin, GROUP)
        p_index = lax.dynamic_slice_in_dim(partner_index, begin, GROUP)
        v_block = lax.dynamic_slice_in_dim(valid, begin, GROUP)
        i_block = lax.dynamic_slice_in_dim(inverse, begin, GROUP)
        scores = SCALE * jnp.dot(q_block, k_block.T, preferred_element_type=jnp.float32)
        p_keys = jnp.take(key_rows, p_index.reshape(-1), axis=0).reshape(GROUP, PARTNERS, D)
        p_logits = SCALE * jnp.einsum('apd,ad->ap', p_keys.astype(jnp.float32), q_block.astype(jnp.float32))
        total = lax.optimization_barrier(jnp.sum(jnp.exp(scores), axis=1)) + lax.optimization_barrier(jnp.sum(jnp.where(v_block, jnp.exp(p_logits), 0.0), axis=1))
        log_total = jnp.log(total)
        loss = log_total - i_block * (jnp.diagonal(scores) + lax.optimization_barrier(jnp.sum(jnp.where(v_block, p_logits, 0.0), axis=1)))
        same = jnp.arange(GROUP, dtype=jnp.int32)[:, None] == jnp.arange(GROUP, dtype=jnp.int32)[None, :]
        weights = (jnp.exp(scores - log_total[:, None]) - jnp.where(same, i_block[:, None], 0.0)).astype(jnp.bfloat16)
        p_weights = jnp.where(v_block, jnp.exp(p_logits - log_total[:, None]) - i_block[:, None], 0.0).astype(jnp.bfloat16)
        grad_unit_q = SCALE * (jnp.dot(weights, k_block, preferred_element_type=jnp.float32) + jnp.einsum('ap,apd->ad', p_weights.astype(jnp.float32), p_keys.astype(jnp.float32)))
        loop_keys = jnp.dot(weights.T, q_block, preferred_element_type=jnp.float32)
        contrib = p_weights.astype(jnp.float32)[:, :, None] * q_block.astype(jnp.float32)[:, None, :]
        carry = carry.at[p_index.reshape(-1)].add(contrib.reshape(-1, D))
        return (carry, (loss, grad_unit_q, loop_keys))
    start = jnp.zeros((ROWS, D), jnp.float32)
    partner_grad, stacked = lax.scan(one_group, start, jnp.arange(group_count, dtype=jnp.int32))
    loss = stacked[0].reshape(ROWS)
    grad_unit_q = stacked[1].reshape(ROWS, D)
    loop_keys = stacked[2].reshape(ROWS, D)
    grad_queries = back_unit(unit_q, norm_q, grad_unit_q)
    grad_keys = back_unit(unit_k, norm_k, SCALE * (loop_keys + partner_grad))
    return (loss, grad_queries, grad_keys)
```

```python
import functools

import jax
import jax.numpy as jnp
import numpy as np
from jax import lax
from jax.experimental import pallas as pl
from jax.experimental.pallas import tpu as pltpu
from jax.sharding import PartitionSpec as P

SCALE = 10.0
EPS = 1e-06
F32 = jnp.float32
BF16 = jnp.bfloat16
VMEM_BYTES = 40 * 1024 * 1024


def chip_ring(chips):
    width = 2 if chips <= 8 else 4
    if chips % width or (chips // width) % 2:
        return list(range(chips))
    height = chips // width
    order = []
    for row in range(height):
        columns = range(1, width) if row % 2 == 0 else range(width - 1, 0, -1)
        order += [row * width + column for column in columns]
    order += [row * width for row in range(height - 1, -1, -1)]
    return order


def call(kernel, outs, operands, flops, smem=(), aliases=None):
    moved = sum(x.size * x.dtype.itemsize for x in operands)
    moved += sum(int(np.prod(o.shape)) * o.dtype.itemsize for o in outs)
    specs = [
        pl.BlockSpec(memory_space=pltpu.SMEM if i in smem else pltpu.VMEM)
        for i in range(len(operands))
    ]
    return pl.pallas_call(
        kernel,
        out_shape=list(outs),
        in_specs=specs,
        out_specs=[pl.BlockSpec(memory_space=pltpu.VMEM)] * len(outs),
        compiler_params=pltpu.CompilerParams(vmem_limit_bytes=VMEM_BYTES),
        cost_estimate=pl.CostEstimate(
            flops=int(flops), bytes_accessed=int(moved), transcendentals=0
        ),
    )(*operands)


def shape(dims, dtype=F32):
    return jax.ShapeDtypeStruct(dims, dtype)


def unit_of(rows):
    wide = rows.astype(F32)
    norms = jnp.sqrt(jnp.sum(wide * wide, axis=1, keepdims=True) + EPS)
    return wide / norms, norms


def back_unit(unit, norms, grad):
    return (grad - unit * jnp.sum(unit * grad, axis=1, keepdims=True)) / norms


def dot_t(a, b):
    return lax.dot_general(a, b, (((1,), (1,)), ((), ())), preferred_element_type=F32)


def dot(a, b):
    return jnp.dot(a, b, preferred_element_type=F32)


def row_ids(rows, columns, offset=0):
    return (lax.broadcasted_iota(jnp.int32, (rows, columns), 0) + offset).astype(F32)


def column_ids(rows, columns, offset=0):
    return (lax.broadcasted_iota(jnp.int32, (rows, columns), 1) + offset).astype(F32)


def unit_kernel(x_ref, whole_ref, first_ref, second_ref):
    unit = unit_of(x_ref[...])[0].astype(BF16)
    half = first_ref.shape[0]
    whole_ref[...] = unit
    first_ref[...] = unit[:half]
    second_ref[...] = unit[half:]


def codes_kernel(me_ref, table_ref, owner_ref, row_ref, count_ref, codes_ref, inverse_ref):
    slots = owner_ref.shape[0]
    count = count_ref[...]
    inverse_ref[...] = 1.0 / (1.0 + count.astype(F32))
    me = me_ref[0]
    for place in range(codes_ref.shape[0]):
        owner = table_ref[me, place]
        code = jnp.full(count.shape, -1, jnp.int32)
        for slot in range(slots):
            here = (owner_ref[slot : slot + 1, :] == owner) & (slot < count)
            code = jnp.where(here, row_ref[slot : slot + 1, :], code)
        codes_ref[place : place + 1, :] = code.astype(F32)


def group_forward_kernel(me_ref, q_ref, keys_ref, total_ref, diag_ref):
    anchors = q_ref.shape[0]
    blocks = keys_ref.shape[0] // anchors
    step = 256
    for start in range(0, anchors, step):
        q = q_ref[start : start + step, :]
        total = jnp.zeros((1, step), F32)
        diag = jnp.zeros((1, step), F32)
        same = row_ids(anchors, step) == column_ids(anchors, step, start)
        for block in range(blocks):
            scores = SCALE * dot_t(keys_ref[block * anchors : (block + 1) * anchors, :], q)
            total += jnp.sum(jnp.exp(scores), axis=0, keepdims=True)
            own = jnp.sum(jnp.where(same, scores, 0.0), axis=0, keepdims=True)
            diag = jnp.where(me_ref[0] == block, own, diag)
        total_ref[:, start : start + step] = total
        diag_ref[:, start : start + step] = diag


def logits_kernel(places, *refs):
    pieces = refs[: len(places)]
    q_ref, s_ref, own_ref, sib_ref, out_ref = refs[len(places) :]
    anchors = q_ref.shape[0]
    step = 256
    order = sorted(set(place for place, _ in places))
    for side, (rows_ref, code_ref) in enumerate(((q_ref, own_ref), (s_ref, sib_ref))):
        for start in range(0, anchors, step):
            q = rows_ref[start : start + step, :]
            for slot, place in enumerate(order):
                code = code_ref[place : place + 1, start : start + step]
                total = jnp.zeros((1, step), F32)
                for (where, offset), piece in zip(places, pieces):
                    if where != place:
                        continue
                    number = piece.shape[0]
                    scores = dot_t(piece[...], q)
                    hit = row_ids(number, step) == code - offset
                    total += jnp.sum(jnp.where(hit, scores, 0.0), axis=0, keepdims=True)
                begin = side * anchors + start
                out_ref[slot : slot + 1, begin : begin + step] = SCALE * total


def totals_kernel(counts, *refs):
    parts = refs[: len(counts)]
    own_ref, sib_ref, group_ref, logits_ref, payload_ref = refs[len(counts) :]
    chips = sib_ref.shape[0]
    anchors = own_ref.shape[1]
    partial = jnp.zeros((1, anchors), F32)
    for part, places in zip(parts, counts):
        for slot, place in enumerate(places):
            logit = part[slot : slot + 1, :anchors]
            logits_ref[place : place + 1, :] = part[slot : slot + 1, :]
            payload_ref[place : place + 1, :] = part[slot : slot + 1, anchors:]
            live = own_ref[place : place + 1, :] >= 0
            partial += jnp.where(live, jnp.exp(logit), 0.0)
    payload_ref[chips : chips + 1, :] = partial + group_ref[...]


def weights_kernel(
    logits_ref,
    payload_ref,
    other_ref,
    own_ref,
    sib_ref,
    inv_ref,
    inv_sib_ref,
    diag_ref,
    loss_ref,
    log_ref,
    weights_ref,
    columns_ref,
    sib_columns_ref,
):
    chips, anchors = sib_ref.shape
    total = payload_ref[chips : chips + 1, :]
    sib_total = other_ref[chips : chips + 1, :]
    chosen = jnp.zeros((1, anchors), F32)
    for place in range(chips):
        here = other_ref[place : place + 1, :]
        live = own_ref[chips + place : chips + place + 1, :] >= 0
        total += jnp.where(live, jnp.exp(here), 0.0)
        chosen += jnp.where(live, here, 0.0)
        live = own_ref[place : place + 1, :] >= 0
        chosen += jnp.where(live, logits_ref[place : place + 1, :anchors], 0.0)
        live = sib_ref[place : place + 1, :] >= 0
        sib_total += jnp.where(live, jnp.exp(logits_ref[place : place + 1, anchors:]), 0.0)
    log_total = jnp.log(total)
    sib_log = jnp.log(sib_total)
    inverse = inv_ref[...]
    loss_ref[...] = log_total - inverse * (diag_ref[...] + chosen)
    log_ref[...] = log_total
    sib_rows = []
    for place in range(chips):
        near = jnp.exp(logits_ref[place : place + 1, :anchors] - log_total) - inverse
        far = jnp.exp(other_ref[place : place + 1, :] - log_total) - inverse
        near = jnp.where(own_ref[place : place + 1, :] >= 0, near, 0.0)
        far = jnp.where(own_ref[chips + place : chips + place + 1, :] >= 0, far, 0.0)
        weights_ref[place : place + 1, :] = near
        weights_ref[chips + place : chips + place + 1, :] = far
        sib = jnp.exp(logits_ref[place : place + 1, anchors:] - sib_log) - inv_sib_ref[...]
        sib_rows.append(jnp.where(sib_ref[place : place + 1, :] >= 0, sib, 0.0))
    own = jnp.concatenate(
        [own_ref[:chips, :], weights_ref[:chips, :], log_total, inverse, jnp.zeros((6, anchors), F32)],
        axis=0,
    )
    columns_ref[...] = own.T
    sib_columns_ref[...] = jnp.concatenate([sib_ref[...]] + sib_rows, axis=0).T


def grad_query_kernel(places, *refs):
    pieces = refs[: len(places)]
    me_ref, q_ref, keys_ref, columns_ref, sib_columns_ref, own_ref, sib_ref = refs[len(places) :]
    anchors = q_ref.shape[0]
    blocks = keys_ref.shape[0] // anchors
    chips = sib_columns_ref.shape[1] // 2
    step = 256

    def partner(columns):
        total = jnp.zeros((step, q_ref.shape[1]), F32)
        for (place, offset), piece in zip(places, pieces):
            number = piece.shape[0]
            code = columns[:, place : place + 1] - offset
            weight = columns[:, chips + place : chips + place + 1]
            spread = jnp.where(code == column_ids(step, number), weight, 0.0).astype(BF16)
            total += dot(spread, piece[...])
        return total

    def turn(index, unused):
        start = pl.multiple_of(index * step, step)
        rows = pl.ds(start, step)
        sib_ref[rows, :] = partner(sib_columns_ref[rows, :])
        columns = columns_ref[rows, :]
        total = partner(columns)
        q = q_ref[rows, :]
        log_total = columns[:, 2 * chips : 2 * chips + 1]
        inverse = columns[:, 2 * chips + 1 : 2 * chips + 2]
        same = row_ids(step, anchors, start) == column_ids(step, anchors)
        for block in range(blocks):
            keys = keys_ref[block * anchors : (block + 1) * anchors, :]
            here = jnp.where(me_ref[0] == block, inverse, 0.0)
            scores = SCALE * dot_t(q, keys)
            weights = jnp.exp(scores - log_total) - jnp.where(same, here, 0.0)
            total += dot(weights.astype(BF16), keys)
        own_ref[rows, :] = total
        return unused

    lax.fori_loop(0, anchors // step, turn, 0)


def finish_kernel(x_ref, own_ref, other_ref, out_ref):
    unit, norms = unit_of(x_ref[...])
    out_ref[...] = back_unit(unit, norms, SCALE * (own_ref[...] + other_ref[...]))


def group_key_kernel(me_ref, k_ref, queries_ref, log_ref, inv_ref, out_ref):
    anchors = k_ref.shape[0]
    blocks = queries_ref.shape[0] // anchors
    step = 256

    def turn(index, unused):
        start = pl.multiple_of(index * step, step)
        rows = pl.ds(start, step)
        total = jnp.zeros((step, k_ref.shape[1]), F32)
        same = row_ids(step, anchors, start) == column_ids(step, anchors)
        for block in range(blocks):
            q = queries_ref[block * anchors : (block + 1) * anchors, :]
            here = jnp.where(me_ref[0] == block, inv_ref[...], 0.0)
            scores = SCALE * dot_t(k_ref[rows, :], q)
            weights = jnp.exp(scores - log_ref[block]) - jnp.where(same, here, 0.0)
            total += dot(weights.astype(BF16), q)
        out_ref[rows, :] = total
        return unused

    lax.fori_loop(0, anchors // step, turn, 0)


def grad_key_kernel(places, carried, *refs):
    pieces = refs[: len(places)]
    rest = refs[len(places) :]
    message_ref = rest[0]
    so_far = rest[1 : 1 + carried]
    own_ref, sib_ref = rest[1 + carried :]
    anchors = own_ref.shape[0]
    step = 256

    def turn(index, unused):
        start = pl.multiple_of(index * step, step)
        rows = pl.ds(start, step)
        for side, out in ((0, own_ref), (1, sib_ref)):
            if side < carried:
                total = so_far[side][rows, :]
            else:
                total = jnp.zeros((step, out.shape[1]), F32)
            for (place, offset), piece in zip(places, pieces):
                number = piece.shape[0]
                code = message_ref[place, side : side + 1, offset : offset + number]
                weight = message_ref[place, 2 + side : 3 + side, offset : offset + number]
                spread = jnp.where(row_ids(step, number, start) == code, weight, 0.0)
                total += dot(spread.astype(BF16), piece[...])
            out[rows, :] = total
        return unused

    lax.fori_loop(0, anchors // step, turn, 0)


def shards(queries, keys, partner_owner, partner_row, partner_count):
    anchors, width = queries.shape
    sky = lax.axis_size("sky")
    loop = lax.axis_size("loop")
    chips = sky // 2
    half = anchors // 2
    order = chip_ring(chips)
    position = {chip: place for place, chip in enumerate(order)}
    table = np.zeros((sky, sky), np.int32)
    for device in range(sky):
        for place in range(chips):
            chip = order[(position[device // 2] - place) % chips]
            table[device, place] = chip * 2 + device % 2
            table[device, chips + place] = chip * 2 + 1 - device % 2
    siblings = [(i, i ^ 1) for i in range(sky)]

    def around(x, shift):
        pairs = []
        for place, chip in enumerate(order):
            other = order[(place + shift) % chips]
            pairs += [(chip * 2 + core, other * 2 + core) for core in range(2)]
        return lax.ppermute(x, "sky", pairs)

    def swap(x):
        return lax.ppermute(x, "sky", siblings)

    def ring(first, second):
        got = {0: [(0, first), (half, second)]}
        right, left = [first, second], [first, second]
        for step in range(1, chips // 2):
            right = [around(x, 1) for x in right]
            left = [around(x, -1) for x in left]
            got[step] = [(0, right[0]), (half, right[1])]
            got[chips - step] = [(0, left[0]), (half, left[1])]
        got[chips // 2] = [(0, around(right[0], 1)), (half, around(left[1], -1))]
        return got

    me = lax.axis_index("sky").reshape(1).astype(jnp.int32)
    place_in_loop = lax.axis_index("loop").reshape(1).astype(jnp.int32)
    block = [shape((anchors, width), BF16), shape((half, width), BF16), shape((half, width), BF16)]
    key_rows, key_a, key_b = call(unit_kernel, block, [keys], 5 * keys.size)
    query_rows, query_a, query_b = call(unit_kernel, block, [queries], 5 * queries.size)
    key_pieces = ring(key_a, key_b)
    query_pieces = ring(query_a, query_b)
    codes, inverse = call(
        codes_kernel,
        [shape((sky, anchors)), shape((1, anchors))],
        [me, jnp.asarray(table), partner_owner.T, partner_row.T, partner_count.reshape(1, anchors)],
        1e6,
        smem=(0, 1),
    )
    sib_queries = swap(query_rows)
    sib_codes = swap(jnp.concatenate([codes[chips:], inverse], axis=0))
    sib_codes, sib_inverse = sib_codes[:chips], sib_codes[chips:]
    group_keys = lax.all_gather(key_rows, "loop", axis=0, tiled=True)
    group_queries = lax.all_gather(query_rows, "loop", axis=0, tiled=True)
    one_block = 2 * anchors * anchors * width
    group_total, diag = call(
        group_forward_kernel,
        [shape((1, anchors))] * 2,
        [place_in_loop, query_rows, group_keys],
        loop * one_block,
        smem=(0,),
    )

    batches = [[0]] + [[s, chips - s] for s in range(1, chips // 2)] + [[chips // 2]]
    batches = [sorted(b) for b in batches]
    parts = []
    for batch in batches:
        places = [(place, offset) for place in batch for offset, _ in key_pieces[place]]
        pieces = [piece for place in batch for _, piece in key_pieces[place]]
        (part,) = call(
            functools.partial(logits_kernel, places),
            [shape((len(batch), 2 * anchors))],
            pieces + [query_rows, sib_queries, codes, sib_codes],
            2 * len(batch) * one_block,
        )
        parts.append(part)
    logits, payload = call(
        functools.partial(totals_kernel, batches),
        [shape((chips, 2 * anchors)), shape((chips + 1, anchors))],
        parts + [codes, sib_codes, group_total],
        1e6,
    )
    other = swap(payload)
    loss, log_total, weights, columns, sib_columns = call(
        weights_kernel,
        [
            shape((1, anchors)),
            shape((1, anchors)),
            shape((sky, anchors)),
            shape((anchors, 2 * chips + 8)),
            shape((anchors, 2 * chips)),
        ],
        [logits, payload, other, codes, sib_codes, inverse, sib_inverse, diag],
        1e6,
    )
    all_log = lax.all_gather(log_total, "loop", axis=0)

    message = jnp.concatenate([codes, weights], axis=0).reshape(4, chips, anchors).transpose(1, 0, 2)
    chip = me[0] // 2
    place_of = jnp.asarray(np.array([position[c] for c in range(chips)], np.int32))
    to_place = (place_of[chip] - place_of) % chips
    from_chip = jnp.asarray(table)[me[0], :chips] // 2
    groups = [[c * 2 + core for c in range(chips)] for core in range(2)]
    arrived = lax.all_to_all(
        jnp.take(message, to_place, axis=0),
        "sky",
        split_axis=0,
        concat_axis=0,
        axis_index_groups=groups,
        tiled=True,
    )
    messages = jnp.take(arrived, from_chip, axis=0)

    places = [(place, offset) for place in range(chips) for offset, _ in key_pieces[place]]
    pieces = [piece for place in range(chips) for _, piece in key_pieces[place]]
    summed_q, sib_summed_q = call(
        functools.partial(grad_query_kernel, places),
        [shape((anchors, width))] * 2,
        pieces + [place_in_loop, query_rows, group_keys, columns, sib_columns],
        (2 * chips + 2 * loop) * one_block,
        smem=(len(pieces),),
    )
    (grad_queries,) = call(
        finish_kernel,
        [shape((anchors, width))],
        [queries, summed_q, swap(sib_summed_q)],
        1e6,
    )
    (group_k,) = call(
        group_key_kernel,
        [shape((anchors, width))],
        [place_in_loop, key_rows, group_queries, all_log, inverse],
        2 * loop * one_block,
        smem=(0,),
    )
    summed_k = [group_k]
    early = [p for p in range(chips) if min(p, chips - p) < chips // 2 - 1]
    late = [p for p in range(chips) if p not in early]
    for batch in (early, late):
        places = [(place, offset) for place in batch for offset, _ in query_pieces[place]]
        pieces = [piece for place in batch for _, piece in query_pieces[place]]
        summed_k = call(
            functools.partial(grad_key_kernel, places, len(summed_k)),
            [shape((anchors, width))] * 2,
            pieces + [messages] + list(summed_k),
            2 * len(batch) * one_block,
        )
    (grad_keys,) = call(
        finish_kernel,
        [shape((anchors, width))],
        [keys, summed_k[0], swap(summed_k[1])],
        1e6,
    )
    return (loss.reshape(anchors), grad_queries, grad_keys)


def solution(mesh):
    in_specs = (
        P(("sky", "loop"), None),
        P(("sky", "loop"), None),
        P(("sky", "loop"), None),
        P(("sky", "loop"), None),
        P(("sky", "loop")),
    )
    out_specs = (P(("sky", "loop")), P(("sky", "loop"), None), P(("sky", "loop"), None))
    return jax.shard_map(shards, mesh=mesh, in_specs=in_specs, out_specs=out_specs, check_vma=False)
```

```python
import functools

import jax
import jax.numpy as jnp
import numpy as np
from jax import lax
from jax.experimental import pallas as pl
from jax.experimental.pallas import tpu as pltpu
from jax.sharding import PartitionSpec as P

SCALE = 10.0
EPS = 1e-06
F32 = jnp.float32
BF16 = jnp.bfloat16
SPARE_BYTES = 6 * 1024 * 1024


def chip_ring(chips):
    width = 2 if chips <= 8 else 4
    if chips % width or (chips // width) % 2:
        return list(range(chips))
    height = chips // width
    order = []
    for row in range(height):
        columns = range(1, width) if row % 2 == 0 else range(width - 1, 0, -1)
        order += [row * width + column for column in columns]
    order += [row * width for row in range(height - 1, -1, -1)]
    return order


def padded(x):
    dims = (1, 1) + tuple(x.shape)
    size = jnp.dtype(x.dtype).itemsize
    rows = 32 // size
    tile = -(-dims[-2] // rows) * rows * -(-dims[-1] // 128) * 128
    return int(np.prod(dims[:-2])) * tile * size


def call(kernel, outs, operands, flops, smem=()):
    moved = sum(padded(x) for x in list(operands) + list(outs))
    specs = [
        pl.BlockSpec(memory_space=pltpu.SMEM if i in smem else pltpu.VMEM)
        for i in range(len(operands))
    ]
    return pl.pallas_call(
        kernel,
        out_shape=list(outs),
        in_specs=specs,
        out_specs=[pl.BlockSpec(memory_space=pltpu.VMEM)] * len(outs),
        compiler_params=pltpu.CompilerParams(vmem_limit_bytes=moved + SPARE_BYTES),
        cost_estimate=pl.CostEstimate(flops=int(flops), bytes_accessed=moved, transcendentals=0),
    )(*operands)


def shape(dims, dtype=F32):
    return jax.ShapeDtypeStruct(dims, dtype)


def unit_of(rows):
    wide = rows.astype(F32)
    norms = jnp.sqrt(jnp.sum(wide * wide, axis=1, keepdims=True) + EPS)
    return wide / norms, norms


def back_unit(unit, norms, grad):
    return (grad - unit * jnp.sum(unit * grad, axis=1, keepdims=True)) / norms


def dot_t(a, b):
    return lax.dot_general(a, b, (((1,), (1,)), ((), ())), preferred_element_type=F32)


def dot(a, b):
    return jnp.dot(a, b, preferred_element_type=F32)


def row_ids(rows, columns, offset=0):
    return (lax.broadcasted_iota(jnp.int32, (rows, columns), 0) + offset).astype(F32)


def column_ids(rows, columns, offset=0):
    return (lax.broadcasted_iota(jnp.int32, (rows, columns), 1) + offset).astype(F32)


def unit_kernel(x_ref, whole_ref, first_ref, second_ref):
    unit = unit_of(x_ref[...])[0].astype(BF16)
    half = first_ref.shape[0]
    whole_ref[...] = unit
    first_ref[...] = unit[:half]
    second_ref[...] = unit[half:]


def codes_kernel(
    me_ref, table_ref, owner_ref, row_ref, count_ref, codes_ref, inverse_ref, payload_ref
):
    slots = owner_ref.shape[0]
    chips = codes_ref.shape[0] // 2
    count = count_ref[...]
    inverse = 1.0 / (1.0 + count.astype(F32))
    inverse_ref[...] = inverse
    payload_ref[chips : chips + 1, :] = inverse
    me = me_ref[0]
    for place in range(2 * chips):
        owner = table_ref[me, place]
        code = jnp.full(count.shape, -1, jnp.int32)
        for slot in range(slots):
            here = (owner_ref[slot : slot + 1, :] == owner) & (slot < count)
            code = jnp.where(here, row_ref[slot : slot + 1, :], code)
        codes_ref[place : place + 1, :] = code.astype(F32)
        if place >= chips:
            payload_ref[place - chips : place - chips + 1, :] = code.astype(F32)


def group_forward_kernel(blocks, *refs):
    keys = refs[:blocks]
    q_ref, total_ref, diag_ref = refs[blocks:]
    anchors = q_ref.shape[0]
    step = 256
    for start in range(0, anchors, step):
        q = q_ref[start : start + step, :]
        total = jnp.zeros((1, step), F32)
        for block in range(blocks):
            scores = SCALE * dot_t(keys[block][...], q)
            total += jnp.sum(jnp.exp(scores), axis=0, keepdims=True)
            if block == 0:
                same = row_ids(anchors, step) == column_ids(anchors, step, start)
                diag = jnp.sum(jnp.where(same, scores, 0.0), axis=0, keepdims=True)
        total_ref[:, start : start + step] = total
        diag_ref[:, start : start + step] = diag


def joined(refs):
    parts = [ref[...] for ref in refs]
    return parts[0] if len(parts) == 1 else jnp.concatenate(parts, axis=0)


def take_blocks(counts, refs):
    blocks, at = [], 0
    for count in counts:
        blocks.append(refs[at : at + count])
        at += count
    return blocks, refs[at:]


def logits_kernel(places, counts, *refs):
    blocks, rest = take_blocks(counts, refs)
    q_ref, s_ref, own_ref, sib_ref, out_ref = rest
    anchors = q_ref.shape[0]
    step = 256
    for slot, (place, block) in enumerate(zip(places, blocks)):
        keys = joined(block)
        for side, (rows_ref, code_ref) in enumerate(((q_ref, own_ref), (s_ref, sib_ref))):
            for start in range(0, anchors, step):
                code = code_ref[place : place + 1, start : start + step]
                scores = dot_t(keys, rows_ref[start : start + step, :])
                hit = row_ids(anchors, step) == code
                total = jnp.sum(jnp.where(hit, scores, 0.0), axis=0, keepdims=True)
                begin = side * anchors + start
                out_ref[slot : slot + 1, begin : begin + step] = SCALE * total


def totals_kernel(batches, *refs):
    parts = refs[: len(batches)]
    own_ref, group_ref, logits_ref, payload_ref = refs[len(batches) :]
    chips = own_ref.shape[0] // 2
    anchors = own_ref.shape[1]
    partial = jnp.zeros((1, anchors), F32)
    for part, places in zip(parts, batches):
        for slot, place in enumerate(places):
            logit = part[slot : slot + 1, :anchors]
            logits_ref[place : place + 1, :] = part[slot : slot + 1, :]
            payload_ref[place : place + 1, :] = part[slot : slot + 1, anchors:]
            live = own_ref[place : place + 1, :] >= 0
            partial += jnp.where(live, jnp.exp(logit), 0.0)
    payload_ref[chips : chips + 1, :] = partial + group_ref[...]


def weights_kernel(
    me_ref,
    table_ref,
    logits_ref,
    payload_ref,
    other_ref,
    own_ref,
    sib_ref,
    inv_ref,
    diag_ref,
    loss_ref,
    log_ref,
    message_ref,
    columns_ref,
    sib_columns_ref,
):
    chips = sib_ref.shape[0] - 1
    anchors = sib_ref.shape[1]
    me = me_ref[0]
    total = payload_ref[chips : chips + 1, :]
    sib_total = other_ref[chips : chips + 1, :]
    chosen = jnp.zeros((1, anchors), F32)
    for place in range(chips):
        here = other_ref[place : place + 1, :]
        live = own_ref[chips + place : chips + place + 1, :] >= 0
        total += jnp.where(live, jnp.exp(here), 0.0)
        chosen += jnp.where(live, here, 0.0)
        live = own_ref[place : place + 1, :] >= 0
        chosen += jnp.where(live, logits_ref[place : place + 1, :anchors], 0.0)
        live = sib_ref[place : place + 1, :] >= 0
        sib_total += jnp.where(live, jnp.exp(logits_ref[place : place + 1, anchors:]), 0.0)
    log_total = jnp.log(total)
    sib_log = jnp.log(sib_total)
    inverse = inv_ref[...]
    sib_inverse = sib_ref[chips : chips + 1, :]
    loss_ref[...] = log_total - inverse * (diag_ref[...] + chosen)
    log_ref[...] = log_total
    own_rows, sib_rows = [], []
    for place in range(chips):
        chip = table_ref[me, place] // 2
        near_code = own_ref[place : place + 1, :]
        far_code = own_ref[chips + place : chips + place + 1, :]
        sib_code = sib_ref[place : place + 1, :]
        near = jnp.exp(logits_ref[place : place + 1, :anchors] - log_total) - inverse
        far = jnp.exp(other_ref[place : place + 1, :] - log_total) - inverse
        sib = jnp.exp(logits_ref[place : place + 1, anchors:] - sib_log) - sib_inverse
        near = jnp.where(near_code >= 0, near, 0.0)
        far = jnp.where(far_code >= 0, far, 0.0)
        own_rows.append(near)
        sib_rows.append(jnp.where(sib_code >= 0, sib, 0.0))
        message_ref[chip] = jnp.concatenate([near_code, far_code, near, far], axis=0)
    filler = jnp.zeros((6, anchors), F32)
    own = [own_ref[:chips, :]] + own_rows + [log_total, inverse, filler]
    columns_ref[...] = jnp.concatenate(own, axis=0).T
    sib_columns_ref[...] = jnp.concatenate([sib_ref[:chips, :]] + sib_rows, axis=0).T


def grad_query_kernel(counts, groups, *refs):
    blocks, rest = take_blocks(counts, refs)
    group_keys, rest = rest[:groups], rest[groups:]
    q_ref, columns_ref, sib_columns_ref, own_ref, sib_ref = rest
    anchors, width = q_ref.shape
    chips = len(counts)
    step = 256

    def partner(columns):
        total = jnp.zeros((step, width), F32)
        for place, block in enumerate(blocks):
            code = columns[:, place : place + 1]
            weight = columns[:, chips + place : chips + place + 1]
            spread = jnp.where(code == column_ids(step, anchors), weight, 0.0).astype(BF16)
            total += dot(spread, joined(block))
        return total

    for start in range(0, anchors, step):
        rows = slice(start, start + step)
        sib_ref[rows, :] = partner(sib_columns_ref[rows, :])
        columns = columns_ref[rows, :]
        total = partner(columns)
        q = q_ref[rows, :]
        log_total = columns[:, 2 * chips : 2 * chips + 1]
        inverse = columns[:, 2 * chips + 1 : 2 * chips + 2]
        for index, keys in enumerate(group_keys):
            scores = SCALE * dot_t(q, keys[...])
            weights = jnp.exp(scores - log_total)
            if index == 0:
                same = row_ids(step, anchors, start) == column_ids(step, anchors)
                weights -= jnp.where(same, inverse, 0.0)
            total += dot(weights.astype(BF16), keys[...])
        own_ref[rows, :] = total


def finish_kernel(x_ref, own_ref, other_ref, out_ref):
    unit, norms = unit_of(x_ref[...])
    out_ref[...] = back_unit(unit, norms, SCALE * (own_ref[...] + other_ref[...]))


def group_key_kernel(groups, *refs):
    queries, logs = refs[:groups], refs[groups : 2 * groups]
    k_ref, inv_ref, out_ref = refs[2 * groups :]
    anchors, width = k_ref.shape
    step = 256
    for start in range(0, anchors, step):
        rows = slice(start, start + step)
        total = jnp.zeros((step, width), F32)
        for index in range(groups):
            q = queries[index][...]
            scores = SCALE * dot_t(k_ref[rows, :], q)
            weights = jnp.exp(scores - logs[index][...])
            if index == 0:
                same = row_ids(step, anchors, start) == column_ids(step, anchors)
                weights -= jnp.where(same, inv_ref[...], 0.0)
            total += dot(weights.astype(BF16), q)
        out_ref[rows, :] = total


def grad_key_kernel(places, counts, carried, me_ref, table_ref, *refs):
    blocks, rest = take_blocks(counts, refs)
    message_ref = rest[0]
    so_far = rest[1 : 1 + carried]
    outs = rest[1 + carried :]
    anchors, width = outs[0].shape
    step = 256
    chip = [table_ref[me_ref[0], place] // 2 for place in places]
    for side, out in enumerate(outs):
        for start in range(0, anchors, step):
            rows = slice(start, start + step)
            total = so_far[side][rows, :] if side < carried else jnp.zeros((step, width), F32)
            for at, block in zip(chip, blocks):
                code = message_ref[at, side : side + 1, :]
                weight = message_ref[at, 2 + side : 3 + side, :]
                spread = jnp.where(row_ids(step, anchors, start) == code, weight, 0.0)
                total += dot(spread.astype(BF16), joined(block))
            out[rows, :] = total


def shards(queries, keys, partner_owner, partner_row, partner_count):
    anchors, width = queries.shape
    sky = lax.axis_size("sky")
    loop = lax.axis_size("loop")
    chips = sky // 2
    half = anchors // 2
    order = chip_ring(chips)
    position = {chip: place for place, chip in enumerate(order)}
    table = np.zeros((sky, sky), np.int32)
    for device in range(sky):
        for place in range(chips):
            chip = order[(position[device // 2] - place) % chips]
            table[device, place] = chip * 2 + device % 2
            table[device, chips + place] = chip * 2 + 1 - device % 2
    siblings = [(i, i ^ 1) for i in range(sky)]

    def around(x, shift):
        pairs = []
        for place, chip in enumerate(order):
            other = order[(place + shift) % chips]
            pairs += [(chip * 2 + core, other * 2 + core) for core in range(2)]
        return lax.ppermute(x, "sky", pairs)

    def swap(x):
        return lax.ppermute(x, "sky", siblings)

    def ring(first, second):
        got = {0: [first, second]}
        right, left = [first, second], [first, second]
        for step in range(1, chips // 2):
            right = [around(x, 1) for x in right]
            left = [around(x, -1) for x in left]
            got[step] = right
            got[chips - step] = left
        got[chips // 2] = [around(right[0], 1), around(left[1], -1)]
        return got

    def group(x):
        shifts = [[(i, (i + s) % loop) for i in range(loop)] for s in range(1, loop)]
        return [x] + [lax.ppermute(x, "loop", pairs) for pairs in shifts]

    me = lax.axis_index("sky").reshape(1).astype(jnp.int32)
    where = [me, jnp.asarray(table)]
    block = [shape((anchors, width), BF16), shape((half, width), BF16), shape((half, width), BF16)]
    one_block = 2 * anchors * anchors * width
    key_rows, key_a, key_b = call(unit_kernel, block, [keys], 5 * keys.size)
    query_rows, query_a, query_b = call(unit_kernel, block, [queries], 5 * queries.size)
    key_pieces = ring(key_a, key_b)
    key_pieces[0] = [key_rows]
    query_pieces = ring(query_a, query_b)
    query_pieces[0] = [query_rows]
    codes, inverse, for_sibling = call(
        codes_kernel,
        [shape((sky, anchors)), shape((1, anchors)), shape((chips + 1, anchors))],
        where + [partner_owner.T, partner_row.T, partner_count.reshape(1, anchors)],
        1e6,
        smem=(0, 1),
    )
    sib_queries = swap(query_rows)
    sib_codes = swap(for_sibling)
    group_keys = group(key_rows)
    group_queries = group(query_rows)
    group_total, diag = call(
        functools.partial(group_forward_kernel, loop),
        [shape((1, anchors))] * 2,
        group_keys + [query_rows],
        loop * one_block,
    )

    def flat(pieces, places):
        return [piece for place in places for piece in pieces[place]]

    batches = [[0]] + [[s, chips - s] for s in range(1, chips // 2)] + [[chips // 2]]
    parts = []
    for batch in batches:
        counts = [len(key_pieces[place]) for place in batch]
        (part,) = call(
            functools.partial(logits_kernel, batch, counts),
            [shape((len(batch), 2 * anchors))],
            flat(key_pieces, batch) + [query_rows, sib_queries, codes, sib_codes],
            2 * len(batch) * one_block,
        )
        parts.append(part)
    logits, payload = call(
        functools.partial(totals_kernel, batches),
        [shape((chips, 2 * anchors)), shape((chips + 1, anchors))],
        parts + [codes, group_total],
        1e6,
    )
    other = swap(payload)
    loss, log_total, message, columns, sib_columns = call(
        weights_kernel,
        [
            shape((1, anchors)),
            shape((1, anchors)),
            shape((chips, 4, anchors)),
            shape((anchors, 2 * chips + 8)),
            shape((anchors, 2 * chips)),
        ],
        where + [logits, payload, other, codes, sib_codes, inverse, diag],
        1e6,
        smem=(0, 1),
    )
    group_logs = group(log_total)

    groups = [[c * 2 + core for c in range(chips)] for core in range(2)]
    messages = lax.all_to_all(
        message, "sky", split_axis=0, concat_axis=0, axis_index_groups=groups, tiled=True
    )
    counts = [len(key_pieces[place]) for place in range(chips)]
    summed_q, sib_summed_q = call(
        functools.partial(grad_query_kernel, counts, loop),
        [shape((anchors, width))] * 2,
        flat(key_pieces, range(chips)) + group_keys + [query_rows, columns, sib_columns],
        (2 * chips + 2 * loop) * one_block,
    )
    (grad_queries,) = call(
        finish_kernel,
        [shape((anchors, width))],
        [queries, summed_q, swap(sib_summed_q)],
        1e6,
    )
    summed_k = call(
        functools.partial(group_key_kernel, loop),
        [shape((anchors, width))],
        group_queries + group_logs + [key_rows, inverse],
        2 * loop * one_block,
    )
    middle = chips // 2
    near = [p for p in range(chips) if min(p, chips - p) < middle - 1]
    for batch in (near, [middle - 1, middle + 1], [middle]):
        counts = [len(query_pieces[place]) for place in batch]
        summed_k = call(
            functools.partial(grad_key_kernel, batch, counts, len(summed_k)),
            [shape((anchors, width))] * 2,
            where + flat(query_pieces, batch) + [messages] + list(summed_k),
            2 * len(batch) * one_block,
            smem=(0, 1),
        )
    (grad_keys,) = call(
        finish_kernel,
        [shape((anchors, width))],
        [keys, summed_k[0], swap(summed_k[1])],
        1e6,
    )
    return (loss.reshape(anchors), grad_queries, grad_keys)


def solution(mesh):
    in_specs = (
        P(("sky", "loop"), None),
        P(("sky", "loop"), None),
        P(("sky", "loop"), None),
        P(("sky", "loop"), None),
        P(("sky", "loop")),
    )
    out_specs = (P(("sky", "loop")), P(("sky", "loop"), None), P(("sky", "loop"), None))
    return jax.shard_map(shards, mesh=mesh, in_specs=in_specs, out_specs=out_specs, check_vma=False)
```

```python
import functools

import jax
import jax.numpy as jnp
import numpy as np
from jax import lax
from jax.experimental import pallas as pl
from jax.experimental.pallas import tpu as pltpu
from jax.sharding import PartitionSpec as P

SCALE = 10.0
EPS = 1e-06
F32 = jnp.float32
BF16 = jnp.bfloat16
COST = 1.0
SPARE_BYTES = 6 * 1024 * 1024


def chip_ring(chips):
    width = 2 if chips <= 8 else 4
    if chips % width or (chips // width) % 2:
        return list(range(chips))
    height = chips // width
    order = []
    for row in range(height):
        columns = range(1, width) if row % 2 == 0 else range(width - 1, 0, -1)
        order += [row * width + column for column in columns]
    order += [row * width for row in range(height - 1, -1, -1)]
    return order


def padded(x):
    dims = (1, 1) + tuple(x.shape)
    size = jnp.dtype(x.dtype).itemsize
    rows = 32 // size
    tile = -(-dims[-2] // rows) * rows * -(-dims[-1] // 128) * 128
    return int(np.prod(dims[:-2])) * tile * size


def call(kernel, outs, operands, flops, smem=()):
    moved = sum(padded(x) for x in list(operands) + list(outs))
    specs = [
        pl.BlockSpec(memory_space=pltpu.SMEM if i in smem else pltpu.VMEM)
        for i in range(len(operands))
    ]
    return pl.pallas_call(
        kernel,
        out_shape=list(outs),
        in_specs=specs,
        out_specs=[pl.BlockSpec(memory_space=pltpu.VMEM)] * len(outs),
        compiler_params=pltpu.CompilerParams(vmem_limit_bytes=moved + SPARE_BYTES),
        cost_estimate=pl.CostEstimate(flops=int(flops * COST), bytes_accessed=int(moved * COST), transcendentals=0),
    )(*operands)


def shape(dims, dtype=F32):
    return jax.ShapeDtypeStruct(dims, dtype)


def unit_of(rows):
    wide = rows.astype(F32)
    norms = jnp.sqrt(jnp.sum(wide * wide, axis=1, keepdims=True) + EPS)
    return wide / norms, norms


def back_unit(unit, norms, grad):
    return (grad - unit * jnp.sum(unit * grad, axis=1, keepdims=True)) / norms


def dot_t(a, b):
    return lax.dot_general(a, b, (((1,), (1,)), ((), ())), preferred_element_type=F32)


def dot(a, b):
    return jnp.dot(a, b, preferred_element_type=F32)


def row_ids(rows, columns, offset=0):
    return (lax.broadcasted_iota(jnp.int32, (rows, columns), 0) + offset).astype(F32)


def column_ids(rows, columns, offset=0):
    return (lax.broadcasted_iota(jnp.int32, (rows, columns), 1) + offset).astype(F32)


def unit_kernel(x_ref, unit_ref):
    unit_ref[...] = unit_of(x_ref[...])[0].astype(BF16)


def unit_both_kernel(x_ref, k_ref, unit_ref, both_ref):
    unit_kernel(x_ref, unit_ref)
    rows = x_ref.shape[0]
    both_ref[:rows, :] = k_ref[...]
    both_ref[rows:, :] = unit_ref[...]


def codes_kernel(
    me_ref, table_ref, owner_ref, row_ref, count_ref, codes_ref, inverse_ref, columns_ref
):
    slots = owner_ref.shape[0]
    places = codes_ref.shape[0] - 1
    count = count_ref[...]
    inverse = 1.0 / (1.0 + count.astype(F32))
    inverse_ref[...] = inverse
    codes_ref[places : places + 1, :] = inverse
    me = me_ref[0]
    for place in range(places):
        owner = table_ref[me, place]
        code = jnp.full(count.shape, -1, jnp.int32)
        for slot in range(slots):
            here = (owner_ref[slot : slot + 1, :] == owner) & (slot < count)
            code = jnp.where(here, row_ref[slot : slot + 1, :], code)
        codes_ref[place : place + 1, :] = code.astype(F32)
    columns_ref[...] = codes_ref[...].T


def group_forward_kernel(groups, k_ref, *refs):
    both = refs[: groups - 1]
    q_ref, total_ref, diag_ref = refs[groups - 1 :]
    anchors = q_ref.shape[0]
    step = 256
    for start in range(0, anchors, step):
        q = q_ref[start : start + step, :]
        total = jnp.zeros((1, step), F32)
        for index in range(groups):
            keys = both[index - 1][:anchors, :] if index else k_ref[...]
            scores = SCALE * dot_t(keys, q)
            total += jnp.sum(jnp.exp(scores), axis=0, keepdims=True)
            if index == 0:
                same = row_ids(anchors, step) == column_ids(anchors, step, start)
                diag = jnp.sum(jnp.where(same, scores, 0.0), axis=0, keepdims=True)
        total_ref[:, start : start + step] = total
        diag_ref[:, start : start + step] = diag


def turn_kernel(rows_ref, columns_ref):
    columns_ref[...] = rows_ref[...].T


def partner_kernel(places, *refs):
    blocks = refs[: len(places)]
    q_ref, s_ref, own_ref, sib_ref, keys_ref, logits_ref = refs[len(places) :]
    anchors = q_ref.shape[0]
    step = 256
    chips = own_ref.shape[1] // 2
    for side, (rows_ref, code_ref) in enumerate(((q_ref, own_ref), (s_ref, sib_ref))):
        for start in range(0, anchors, step):
            rows = slice(start, start + step)
            here = slice(side * anchors + start, side * anchors + start + step)
            q = rows_ref[rows, :].astype(F32)
            logits = []
            for slot, (place, block) in enumerate(zip(places, blocks)):
                at = side * chips + place
                code = code_ref[rows, at : at + 1]
                hot = jnp.where(code == column_ids(step, anchors), 1.0, 0.0).astype(BF16)
                named = dot(hot, block[...])
                keys_ref[slot, here, :] = named.astype(BF16)
                logits.append(SCALE * jnp.sum(named * q, axis=1, keepdims=True))
            logits_ref[here, :] = jnp.concatenate(logits, axis=1)


def totals_kernel(*refs):
    parts = refs[:-3]
    group_ref, logits_ref, payload_ref = refs[-3:]
    anchors = group_ref.shape[1]
    turned = jnp.concatenate([part[...] for part in parts], axis=1).T
    chips = turned.shape[0]
    logits_ref[...] = turned
    payload_ref[:chips, :] = turned[:, anchors:]
    payload_ref[chips : 2 * chips, :] = turned[:, :anchors]
    payload_ref[2 * chips :, :] = group_ref[...]


def weights_kernel(
    me_ref,
    table_ref,
    logits_ref,
    other_ref,
    own_ref,
    sib_ref,
    group_ref,
    diag_ref,
    loss_ref,
    log_ref,
    message_ref,
    columns_ref,
    sib_columns_ref,
):
    chips, anchors = logits_ref.shape[0], group_ref.shape[1]
    me = me_ref[0]

    def all_weights(near, far, near_codes, far_codes, group, inverse):
        total, chosen = group, jnp.zeros((1, anchors), F32)
        for logits, codes in ((near, near_codes), (far, far_codes)):
            live = codes >= 0
            total += jnp.sum(jnp.where(live, jnp.exp(logits), 0.0), axis=0, keepdims=True)
            chosen += jnp.sum(jnp.where(live, logits, 0.0), axis=0, keepdims=True)
        log_total = jnp.log(total)
        near, far = (
            jnp.where(codes >= 0, jnp.exp(logits - log_total) - inverse, 0.0)
            for logits, codes in ((near, near_codes), (far, far_codes))
        )
        return log_total, chosen, near, far

    inverse = own_ref[2 * chips :, :]
    near_code, far_code = own_ref[:chips, :], own_ref[chips : 2 * chips, :]
    sib_near_code, sib_far_code = sib_ref[chips : 2 * chips, :], sib_ref[:chips, :]
    log_total, chosen, near, far = all_weights(
        logits_ref[:, :anchors],
        other_ref[:chips, :],
        near_code,
        far_code,
        group_ref[...],
        inverse,
    )
    loss_ref[...] = log_total - inverse * (diag_ref[...] + chosen)
    log_ref[...] = log_total
    unused, unused, sib_near, sib_far = all_weights(
        logits_ref[:, anchors:],
        other_ref[chips : 2 * chips, :],
        sib_near_code,
        sib_far_code,
        other_ref[2 * chips :, :],
        sib_ref[2 * chips :, :],
    )
    filler = jnp.zeros((6, anchors), F32)
    columns_ref[...] = jnp.concatenate([near, log_total, inverse, filler], axis=0).T
    sib_columns_ref[...] = sib_near.T

    def row(x, slot):
        return x[slot : slot + 1, :]

    message_ref[...] = jnp.zeros_like(message_ref)
    for slot in (0, chips - 1):
        there = table_ref[me, 3 * chips + slot]
        rows = [row(near_code, slot), row(far_code, slot), row(near, slot), row(far, slot)]
        message_ref[there, :4, :] = jnp.concatenate(rows, axis=0)
    for slot in range(2, chips - 1, 2):
        there = table_ref[me, 3 * chips + slot]
        rows = []
        for codes, weights in ((far_code, far), (sib_far_code, sib_far)):
            rows += [row(codes, slot), row(codes, slot - 1)]
            rows += [row(weights, slot), row(weights, slot - 1)]
        message_ref[there] = jnp.concatenate(rows, axis=0)


def partner_sum(columns, order, named, rows):
    total = None
    for place, (ref, slot) in zip(order, named):
        weight = columns[:, place : place + 1].astype(BF16).astype(F32)
        term = weight * ref[slot, rows, :].astype(F32)
        total = term if total is None else total + term
    return total


def named_rows(batches, refs):
    named = [(ref, slot) for ref, places in zip(refs, batches) for slot in range(len(places))]
    return [place for places in batches for place in places], named


def grad_sibling_kernel(batches, *refs):
    order, named = named_rows(batches, refs)
    columns_ref, out_ref = refs[len(batches) :]
    anchors = out_ref.shape[0]
    step = 256
    for start in range(0, anchors, step):
        rows = slice(start, start + step)
        far = slice(anchors + start, anchors + start + step)
        out_ref[rows, :] = partner_sum(columns_ref[rows, :], order, named, far)


def grad_query_kernel(batches, groups, *refs):
    order, named = named_rows(batches, refs)
    rest = refs[len(batches) :]
    k_ref, rest = rest[0], rest[1:]
    both, rest = rest[: groups - 1], rest[groups - 1 :]
    q_ref, columns_ref, out_ref = rest
    anchors = q_ref.shape[0]
    chips = len(order)
    step = 256
    for start in range(0, anchors, step):
        rows = slice(start, start + step)
        columns = columns_ref[rows, :]
        total = partner_sum(columns, order, named, rows)
        q = q_ref[rows, :]
        log_total = columns[:, chips : chips + 1]
        inverse = columns[:, chips + 1 : chips + 2]
        for index in range(groups):
            keys = both[index - 1][:anchors, :] if index else k_ref[...]
            scores = SCALE * dot_t(q, keys)
            weights = jnp.exp(scores - log_total)
            if index == 0:
                same = row_ids(step, anchors, start) == column_ids(step, anchors)
                weights -= jnp.where(same, inverse, 0.0)
            total += dot(weights.astype(BF16), keys)
        out_ref[rows, :] = total


def finish_kernel(x_ref, own_ref, other_ref, out_ref):
    unit, norms = unit_of(x_ref[...])
    out_ref[...] = back_unit(unit, norms, SCALE * (own_ref[...] + other_ref[...]))


def group_key_kernel(groups, *refs):
    q_ref, both, logs = refs[0], refs[1:groups], refs[groups : 2 * groups]
    k_ref, inv_ref, out_ref = refs[2 * groups :]
    anchors, width = k_ref.shape
    step = 256
    for start in range(0, anchors, step):
        rows = slice(start, start + step)
        total = jnp.zeros((step, width), F32)
        for index in range(groups):
            q = both[index - 1][anchors:, :] if index else q_ref[...]
            scores = SCALE * dot_t(k_ref[rows, :], q)
            weights = jnp.exp(scores - logs[index][...])
            if index == 0:
                same = row_ids(step, anchors, start) == column_ids(step, anchors)
                weights -= jnp.where(same, inv_ref[...], 0.0)
            total += dot(weights.astype(BF16), q)
        out_ref[rows, :] = total


def grad_key_kernel(places, carried, me_ref, table_ref, *refs):
    blocks, rest = refs[: len(places)], refs[len(places) :]
    message_ref = rest[0]
    so_far = rest[1 : 1 + carried]
    outs = rest[1 + carried :]
    anchors, width = outs[0].shape
    chips = message_ref.shape[0]
    step = 256
    source = [table_ref[me_ref[0], 2 * chips + place] for place in places]
    first = [4 if place % 2 == 0 and place else 0 for place in places]
    for side, out in enumerate(outs):
        for start in range(0, anchors, step):
            rows = slice(start, start + step)
            total = so_far[side][rows, :] if side < carried else jnp.zeros((step, width), F32)
            for at, base, block in zip(source, first, blocks):
                code = message_ref[at, base + side : base + side + 1, :]
                weight = message_ref[at, base + 2 + side : base + 3 + side, :]
                spread = jnp.where(row_ids(step, anchors, start) == code, weight, 0.0)
                total += dot(spread.astype(BF16), block[...])
            out[rows, :] = total


def shards(queries, keys, partner_owner, partner_row, partner_count):
    anchors, width = queries.shape
    sky = lax.axis_size("sky")
    loop = lax.axis_size("loop")
    chips = sky // 2
    middle = chips // 2
    bits = chips.bit_length() - 1
    order = chip_ring(chips)
    position = {chip: place for place, chip in enumerate(order)}

    def handled(device):
        chip, core = divmod(device, 2)
        way = 1 if core else -1
        along = [order[(position[chip] + way * step) % chips] for step in range(middle + 1)]
        owners = [device]
        for step in range(1, middle):
            owners += [2 * along[step] + core, 2 * along[step] + 1 - core]
        return owners + [2 * along[middle] + core]

    table = np.zeros((sky, 4 * chips), np.int32)
    for device in range(sky):
        near, far = handled(device), handled(device ^ 1)
        for slot in range(chips):
            relative = near[slot] // 2 ^ device // 2
            table[device, slot] = near[slot]
            table[device, chips + slot] = far[slot]
            table[device, 2 * chips + slot] = sum(
                (relative >> bit & 1) << (bits - 1 - bit) for bit in range(bits)
            )
            table[device, 3 * chips + slot] = far[slot] // 2 ^ device // 2
    siblings = [(i, i ^ 1) for i in range(sky)]
    onward = []
    for place, chip in enumerate(order):
        onward.append((chip * 2, order[(place + 1) % chips] * 2))
        onward.append((chip * 2 + 1, order[place - 1] * 2 + 1))

    def swap(x):
        return lax.ppermute(x, "sky", siblings)

    def exchange(message):
        held = message[None]
        stages = []
        step = chips // 2
        while step:
            pairs = [(i, i ^ (2 * step)) for i in range(sky)]
            got = lax.ppermute(held[:, step:], "sky", pairs)
            stages.append(got)
            held = jnp.concatenate([held[:, :step], got], axis=0)
            step //= 2
        return stages, held.reshape(message.shape)

    def after(x, *others):
        return lax.optimization_barrier((x,) + others)[0] if others else x

    class Ring:
        def __init__(self, own, sibling):
            self.front = [own, sibling]
            self.blocks = [own]

        def hop(self, which, *pins):
            self.front[which] = lax.ppermute(after(self.front[which], *pins), "sky", onward)
            self.blocks.append(self.front[which])

    def group(x):
        shifts = [[(i, (i + s) % loop) for i in range(loop)] for s in range(1, loop)]
        return [lax.ppermute(x, "loop", pairs) for pairs in shifts]

    me = lax.axis_index("sky").reshape(1).astype(jnp.int32)
    where = [me, jnp.asarray(table)]
    block = shape((anchors, width), BF16)
    one_block = 2 * anchors * anchors * width
    (key_rows,) = call(unit_kernel, [block], [keys], 5 * keys.size)
    key_ring = Ring(key_rows, swap(key_rows))
    key_ring.hop(0)
    query_rows, both = call(
        unit_both_kernel,
        [block, shape((2 * anchors, width), BF16)],
        [queries, key_rows],
        5 * queries.size,
    )
    key_ring.hop(1)
    sib_queries = swap(query_rows)
    query_ring = Ring(query_rows, sib_queries)
    others = group(both)
    codes, inverse, code_columns = call(
        codes_kernel,
        [shape((sky + 1, anchors)), shape((1, anchors)), shape((anchors, sky + 1))],
        where + [partner_owner.T, partner_row.T, partner_count.reshape(1, anchors)],
        1e6,
        smem=(0, 1),
    )
    sib_codes = swap(codes)
    (sib_code_columns,) = call(turn_kernel, [shape((anchors, sky + 1))], [sib_codes], 1e6)

    def partners_of(batch, *pins):
        return call(
            functools.partial(partner_kernel, batch),
            [shape((len(batch), 2 * anchors, width), BF16), shape((2 * anchors, len(batch)))],
            [key_ring.blocks[place] for place in batch]
            + [after(query_rows, *pins), sib_queries, code_columns, sib_code_columns],
            2 * len(batch) * one_block,
        )

    batches = [[0]] + [[2 * s - 1, 2 * s] for s in range(1, middle)] + [[chips - 1]]
    parts = []
    group_total = diag = None
    pins = ()
    for step in range(2, middle + 1):
        incoming = key_ring.front[0]
        key_ring.hop(0, *pins)
        if step == 2:
            parts.append(partners_of(batches[0]))
            pins = (parts[-1][1],)
        elif group_total is None:
            group_total, diag = call(
                functools.partial(group_forward_kernel, loop),
                [shape((1, anchors))] * 2,
                [key_rows] + others + [after(query_rows, *pins)],
                loop * one_block,
            )
            pins = (group_total,)
        if step < middle:
            key_ring.hop(1, *pins)
            parts.append(partners_of(batches[step - 1], *pins))
            pins = (parts[-1][1],)
    query_ring.hop(0, incoming)
    parts.append(partners_of(batches[middle - 1], *pins))
    query_ring.hop(1, parts[-1][1])
    parts.append(partners_of(batches[middle], parts[-1][1]))
    logits, payload = call(
        totals_kernel,
        [shape((chips, 2 * anchors)), shape((2 * chips + 1, anchors))],
        [part[1] for part in parts] + [group_total],
        1e6,
    )
    query_ring.hop(0, logits)
    other = swap(payload)
    loss, log_total, message, columns, sib_columns = call(
        weights_kernel,
        [
            shape((1, anchors)),
            shape((1, anchors)),
            shape((chips, 8, anchors)),
            shape((anchors, chips + 8)),
            shape((anchors, chips)),
        ],
        where + [logits, other, codes, sib_codes, group_total, diag],
        1e6,
        smem=(0, 1),
    )
    stages, messages = exchange(message)
    all_logs = [log_total] + group(log_total)
    query_ring.hop(1, log_total)
    for step in range(3, middle):
        if step < middle - 1:
            query_ring.hop(0)
            query_ring.hop(1)
    (sib_summed_q,) = call(
        functools.partial(grad_sibling_kernel, batches),
        [shape((anchors, width))],
        [part[0] for part in parts] + [sib_columns],
        1e6,
    )
    query_ring.hop(0, sib_summed_q)
    (summed_q,) = call(
        functools.partial(grad_query_kernel, batches, loop),
        [shape((anchors, width))],
        [part[0] for part in parts]
        + [key_rows]
        + others
        + [after(query_rows, stages[0], sib_summed_q), columns],
        2 * loop * one_block,
    )
    query_ring.hop(1, summed_q)
    (group_k,) = call(
        functools.partial(group_key_kernel, loop),
        [shape((anchors, width))],
        [query_rows] + others + all_logs + [after(key_rows, stages[1], summed_q), inverse],
        2 * loop * one_block,
    )
    query_ring.hop(0, group_k)
    (grad_queries,) = call(
        finish_kernel,
        [shape((anchors, width))],
        [queries, summed_q, swap(sib_summed_q)],
        1e6,
    )
    summed_k = [group_k]
    for batch in (range(chips - 3), [chips - 3, chips - 2], [chips - 1]):
        summed_k = call(
            functools.partial(grad_key_kernel, list(batch), len(summed_k)),
            [shape((anchors, width))] * 2,
            where + [query_ring.blocks[p] for p in batch] + [messages] + list(summed_k),
            2 * len(batch) * one_block,
            smem=(0, 1),
        )
    (grad_keys,) = call(
        finish_kernel,
        [shape((anchors, width))],
        [keys, summed_k[0], swap(summed_k[1])],
        1e6,
    )
    return (loss.reshape(anchors), grad_queries, grad_keys)


def solution(mesh):
    in_specs = (
        P(("sky", "loop"), None),
        P(("sky", "loop"), None),
        P(("sky", "loop"), None),
        P(("sky", "loop"), None),
        P(("sky", "loop")),
    )
    out_specs = (P(("sky", "loop")), P(("sky", "loop"), None), P(("sky", "loop"), None))
    return jax.shard_map(shards, mesh=mesh, in_specs=in_specs, out_specs=out_specs, check_vma=False)
```

```python
import functools

import jax
import jax.numpy as jnp
import numpy as np
from jax import lax
from jax.experimental import pallas as pl
from jax.experimental.pallas import tpu as pltpu
from jax.sharding import PartitionSpec as P

SCALE = 10.0
EPS = 1e-06
F32 = jnp.float32
BF16 = jnp.bfloat16
COST = 1.0
SPARE_BYTES = 6 * 1024 * 1024


def chip_ring(chips):
    width = 2 if chips <= 8 else 4
    if chips % width or (chips // width) % 2:
        return list(range(chips))
    height = chips // width
    order = []
    for row in range(height):
        columns = range(1, width) if row % 2 == 0 else range(width - 1, 0, -1)
        order += [row * width + column for column in columns]
    order += [row * width for row in range(height - 1, -1, -1)]
    return order


def padded(x):
    dims = (1, 1) + tuple(x.shape)
    size = jnp.dtype(x.dtype).itemsize
    rows = 32 // size
    tile = -(-dims[-2] // rows) * rows * -(-dims[-1] // 128) * 128
    return int(np.prod(dims[:-2])) * tile * size


def call(kernel, outs, operands, flops, smem=()):
    moved = sum(padded(x) for x in list(operands) + list(outs))
    specs = [
        pl.BlockSpec(memory_space=pltpu.SMEM if i in smem else pltpu.VMEM)
        for i in range(len(operands))
    ]
    return pl.pallas_call(
        kernel,
        out_shape=list(outs),
        in_specs=specs,
        out_specs=[pl.BlockSpec(memory_space=pltpu.VMEM)] * len(outs),
        compiler_params=pltpu.CompilerParams(vmem_limit_bytes=moved + SPARE_BYTES),
        cost_estimate=pl.CostEstimate(flops=int(flops * COST), bytes_accessed=int(moved * COST), transcendentals=0),
    )(*operands)


def shape(dims, dtype=F32):
    return jax.ShapeDtypeStruct(dims, dtype)


def unit_of(rows):
    wide = rows.astype(F32)
    norms = jnp.sqrt(jnp.sum(wide * wide, axis=1, keepdims=True) + EPS)
    return wide / norms, norms


def back_unit(unit, norms, grad):
    return (grad - unit * jnp.sum(unit * grad, axis=1, keepdims=True)) / norms


def dot_t(a, b):
    return lax.dot_general(a, b, (((1,), (1,)), ((), ())), preferred_element_type=F32)


def dot(a, b):
    return jnp.dot(a, b, preferred_element_type=F32)


def row_ids(rows, columns, offset=0):
    return (lax.broadcasted_iota(jnp.int32, (rows, columns), 0) + offset).astype(F32)


def column_ids(rows, columns, offset=0):
    return (lax.broadcasted_iota(jnp.int32, (rows, columns), 1) + offset).astype(F32)


def unit_kernel(x_ref, unit_ref):
    unit_ref[...] = unit_of(x_ref[...])[0].astype(BF16)


def unit_both_kernel(x_ref, k_ref, unit_ref, both_ref):
    unit_kernel(x_ref, unit_ref)
    rows = x_ref.shape[0]
    both_ref[:rows, :] = k_ref[...]
    both_ref[rows:, :] = unit_ref[...]


def codes_kernel(
    me_ref, table_ref, owner_ref, row_ref, count_ref, codes_ref, inverse_ref, columns_ref
):
    slots = owner_ref.shape[0]
    places = codes_ref.shape[0] - 1
    count = count_ref[...]
    inverse = 1.0 / (1.0 + count.astype(F32))
    inverse_ref[...] = inverse
    codes_ref[places : places + 1, :] = inverse
    me = me_ref[0]
    for place in range(places):
        owner = table_ref[me, place]
        code = jnp.full(count.shape, -1, jnp.int32)
        for slot in range(slots):
            here = (owner_ref[slot : slot + 1, :] == owner) & (slot < count)
            code = jnp.where(here, row_ref[slot : slot + 1, :], code)
        codes_ref[place : place + 1, :] = code.astype(F32)
    columns_ref[...] = codes_ref[...].T


def group_forward_kernel(groups, k_ref, *refs):
    both = refs[: groups - 1]
    q_ref, total_ref, diag_ref = refs[groups - 1 :]
    anchors = q_ref.shape[0]
    step = 256
    for start in range(0, anchors, step):
        q = q_ref[start : start + step, :]
        total = jnp.zeros((1, step), F32)
        for index in range(groups):
            keys = both[index - 1][:anchors, :] if index else k_ref[...]
            scores = SCALE * dot_t(keys, q)
            total += jnp.sum(jnp.exp(scores), axis=0, keepdims=True)
            if index == 0:
                same = row_ids(anchors, step) == column_ids(anchors, step, start)
                diag = jnp.sum(jnp.where(same, scores, 0.0), axis=0, keepdims=True)
        total_ref[:, start : start + step] = total
        diag_ref[:, start : start + step] = diag


def turn_kernel(rows_ref, columns_ref):
    columns_ref[...] = rows_ref[...].T


def partner_kernel(places, *refs):
    blocks = refs[: len(places)]
    q_ref, s_ref, own_ref, sib_ref, keys_ref, logits_ref = refs[len(places) :]
    anchors = q_ref.shape[0]
    step = 256
    chips = own_ref.shape[1] // 2
    for side, (rows_ref, code_ref) in enumerate(((q_ref, own_ref), (s_ref, sib_ref))):
        for start in range(0, anchors, step):
            rows = slice(start, start + step)
            here = slice(side * anchors + start, side * anchors + start + step)
            q = rows_ref[rows, :].astype(F32)
            logits = []
            for slot, (place, block) in enumerate(zip(places, blocks)):
                at = side * chips + place
                code = code_ref[rows, at : at + 1]
                hot = jnp.where(code == column_ids(step, anchors), 1.0, 0.0).astype(BF16)
                named = dot(hot, block[...])
                keys_ref[slot, here, :] = named.astype(BF16)
                logits.append(SCALE * jnp.sum(named * q, axis=1, keepdims=True))
            logits_ref[here, :] = jnp.concatenate(logits, axis=1)


def totals_kernel(*refs):
    parts = refs[:-3]
    group_ref, logits_ref, payload_ref = refs[-3:]
    anchors = group_ref.shape[1]
    turned = jnp.concatenate([part[...] for part in parts], axis=1).T
    chips = turned.shape[0]
    logits_ref[...] = turned
    payload_ref[:chips, :] = turned[:, anchors:]
    payload_ref[chips : 2 * chips, :] = turned[:, :anchors]
    payload_ref[2 * chips :, :] = group_ref[...]


def weights_kernel(
    logits_ref,
    other_ref,
    own_ref,
    sib_ref,
    group_ref,
    diag_ref,
    loss_ref,
    log_ref,
    home_ref,
    message_ref,
    columns_ref,
    sib_columns_ref,
):
    chips, anchors = logits_ref.shape[0], group_ref.shape[1]

    def all_weights(near, far, near_codes, far_codes, group, inverse):
        total, chosen = group, jnp.zeros((1, anchors), F32)
        for logits, codes in ((near, near_codes), (far, far_codes)):
            live = codes >= 0
            total += jnp.sum(jnp.where(live, jnp.exp(logits), 0.0), axis=0, keepdims=True)
            chosen += jnp.sum(jnp.where(live, logits, 0.0), axis=0, keepdims=True)
        log_total = jnp.log(total)
        near, far = (
            jnp.where(codes >= 0, jnp.exp(logits - log_total) - inverse, 0.0)
            for logits, codes in ((near, near_codes), (far, far_codes))
        )
        return log_total, chosen, near, far

    inverse = own_ref[2 * chips :, :]
    near_code, far_code = own_ref[:chips, :], own_ref[chips : 2 * chips, :]
    sib_near_code, sib_far_code = sib_ref[chips : 2 * chips, :], sib_ref[:chips, :]
    log_total, chosen, near, far = all_weights(
        logits_ref[:, :anchors],
        other_ref[:chips, :],
        near_code,
        far_code,
        group_ref[...],
        inverse,
    )
    loss_ref[...] = log_total - inverse * (diag_ref[...] + chosen)
    log_ref[...] = log_total
    unused, unused, sib_near, sib_far = all_weights(
        logits_ref[:, anchors:],
        other_ref[chips : 2 * chips, :],
        sib_near_code,
        sib_far_code,
        other_ref[2 * chips :, :],
        sib_ref[2 * chips :, :],
    )
    filler = jnp.zeros((6, anchors), F32)
    columns_ref[...] = jnp.concatenate([near, log_total, inverse, filler], axis=0).T
    sib_columns_ref[...] = sib_near.T

    def row(x, slot):
        return x[slot : slot + 1, :]

    def both_sides(slot):
        return [row(near_code, slot), row(far_code, slot), row(near, slot), row(far, slot)]

    home_ref[:4, :] = jnp.concatenate(both_sides(0), axis=0)
    home_ref[4:, :] = jnp.zeros((4, anchors), F32)
    for slot in range(2, chips - 1, 2):
        rows = []
        for codes, weights in ((far_code, far), (sib_far_code, sib_far)):
            rows += [row(codes, slot), row(codes, slot - 1)]
            rows += [row(weights, slot), row(weights, slot - 1)]
        message_ref[slot // 2 - 1] = jnp.concatenate(rows, axis=0)
    last = both_sides(chips - 1) + [jnp.zeros((4, anchors), F32)]
    message_ref[chips // 2 - 1] = jnp.concatenate(last, axis=0)


def partner_sum(columns, order, named, rows):
    total = None
    for place, (ref, slot) in zip(order, named):
        weight = columns[:, place : place + 1].astype(BF16).astype(F32)
        term = weight * ref[slot, rows, :].astype(F32)
        total = term if total is None else total + term
    return total


def named_rows(batches, refs):
    named = [(ref, slot) for ref, places in zip(refs, batches) for slot in range(len(places))]
    return [place for places in batches for place in places], named


def grad_sibling_kernel(batches, *refs):
    order, named = named_rows(batches, refs)
    columns_ref, out_ref = refs[len(batches) :]
    anchors = out_ref.shape[0]
    step = 256
    for start in range(0, anchors, step):
        rows = slice(start, start + step)
        far = slice(anchors + start, anchors + start + step)
        out_ref[rows, :] = partner_sum(columns_ref[rows, :], order, named, far)


def grad_query_kernel(batches, groups, *refs):
    order, named = named_rows(batches, refs)
    rest = refs[len(batches) :]
    k_ref, rest = rest[0], rest[1:]
    both, rest = rest[: groups - 1], rest[groups - 1 :]
    q_ref, columns_ref, out_ref = rest
    anchors = q_ref.shape[0]
    chips = len(order)
    step = 256
    for start in range(0, anchors, step):
        rows = slice(start, start + step)
        columns = columns_ref[rows, :]
        total = partner_sum(columns, order, named, rows)
        q = q_ref[rows, :]
        log_total = columns[:, chips : chips + 1]
        inverse = columns[:, chips + 1 : chips + 2]
        for index in range(groups):
            keys = both[index - 1][:anchors, :] if index else k_ref[...]
            scores = SCALE * dot_t(q, keys)
            weights = jnp.exp(scores - log_total)
            if index == 0:
                same = row_ids(step, anchors, start) == column_ids(step, anchors)
                weights -= jnp.where(same, inverse, 0.0)
            total += dot(weights.astype(BF16), keys)
        out_ref[rows, :] = total


def finish_kernel(x_ref, own_ref, other_ref, out_ref):
    unit, norms = unit_of(x_ref[...])
    out_ref[...] = back_unit(unit, norms, SCALE * (own_ref[...] + other_ref[...]))


def group_key_kernel(groups, *refs):
    q_ref, both, logs = refs[0], refs[1:groups], refs[groups : 2 * groups]
    k_ref, inv_ref, out_ref = refs[2 * groups :]
    anchors, width = k_ref.shape
    step = 256
    for start in range(0, anchors, step):
        rows = slice(start, start + step)
        total = jnp.zeros((step, width), F32)
        for index in range(groups):
            q = both[index - 1][anchors:, :] if index else q_ref[...]
            scores = SCALE * dot_t(k_ref[rows, :], q)
            weights = jnp.exp(scores - logs[index][...])
            if index == 0:
                same = row_ids(step, anchors, start) == column_ids(step, anchors)
                weights -= jnp.where(same, inv_ref[...], 0.0)
            total += dot(weights.astype(BF16), q)
        out_ref[rows, :] = total


def grad_key_kernel(sources, blocks, carried, *refs):
    queries, messages = refs[:blocks], refs[blocks : -2 - carried]
    so_far, outs = refs[len(refs) - 2 - carried : len(refs) - 2], refs[-2:]
    anchors, width = outs[0].shape
    step = 256
    for side, out in enumerate(outs):
        for start in range(0, anchors, step):
            rows = slice(start, start + step)
            total = so_far[side][rows, :] if side < carried else jnp.zeros((step, width), F32)
            for (at, base), block in zip(sources, queries):
                code = messages[at][base + side : base + side + 1, :]
                weight = messages[at][base + 2 + side : base + 3 + side, :]
                spread = jnp.where(row_ids(step, anchors, start) == code, weight, 0.0)
                total += dot(spread.astype(BF16), block[...])
            out[rows, :] = total


def shards(queries, keys, partner_owner, partner_row, partner_count):
    anchors, width = queries.shape
    sky = lax.axis_size("sky")
    loop = lax.axis_size("loop")
    chips = sky // 2
    middle = chips // 2
    order = chip_ring(chips)
    position = {chip: place for place, chip in enumerate(order)}

    def handled(device):
        chip, core = divmod(device, 2)
        way = 1 if core else -1
        along = [order[(position[chip] + way * step) % chips] for step in range(middle + 1)]
        owners = [device]
        for step in range(1, middle):
            owners += [2 * along[step] + core, 2 * along[step] + 1 - core]
        return owners + [2 * along[middle] + core]

    table = np.array([handled(device) + handled(device ^ 1) for device in range(sky)], np.int32)
    siblings = [(i, i ^ 1) for i in range(sky)]
    onward = []
    for place, chip in enumerate(order):
        onward.append((chip * 2, order[(place + 1) % chips] * 2))
        onward.append((chip * 2 + 1, order[place - 1] * 2 + 1))

    def swap(x):
        return lax.ppermute(x, "sky", siblings)

    def after(x, *others):
        return lax.optimization_barrier((x,) + others)[0] if others else x

    class Ring:
        def __init__(self, own, sibling):
            self.front = [own, sibling]
            self.blocks = [own]

        def hop(self, which, *pins):
            self.front[which] = lax.ppermute(after(self.front[which], *pins), "sky", onward)
            self.blocks.append(self.front[which])

    def group(x):
        shifts = [[(i, (i + s) % loop) for i in range(loop)] for s in range(1, loop)]
        return [lax.ppermute(x, "loop", pairs) for pairs in shifts]

    me = lax.axis_index("sky").reshape(1).astype(jnp.int32)
    where = [me, jnp.asarray(table)]
    block = shape((anchors, width), BF16)
    one_block = 2 * anchors * anchors * width
    (key_rows,) = call(unit_kernel, [block], [keys], 5 * keys.size)
    key_ring = Ring(key_rows, swap(key_rows))
    key_ring.hop(0)
    query_rows, both = call(
        unit_both_kernel,
        [block, shape((2 * anchors, width), BF16)],
        [queries, key_rows],
        5 * queries.size,
    )
    key_ring.hop(1)
    sib_queries = swap(query_rows)
    query_ring = Ring(query_rows, sib_queries)
    others = group(both)
    codes, inverse, code_columns = call(
        codes_kernel,
        [shape((sky + 1, anchors)), shape((1, anchors)), shape((anchors, sky + 1))],
        where + [partner_owner.T, partner_row.T, partner_count.reshape(1, anchors)],
        1e6,
        smem=(0, 1),
    )
    sib_codes = swap(codes)
    (sib_code_columns,) = call(turn_kernel, [shape((anchors, sky + 1))], [sib_codes], 1e6)

    def partners_of(batch, *pins):
        return call(
            functools.partial(partner_kernel, batch),
            [shape((len(batch), 2 * anchors, width), BF16), shape((2 * anchors, len(batch)))],
            [key_ring.blocks[place] for place in batch]
            + [after(query_rows, *pins), sib_queries, code_columns, sib_code_columns],
            2 * len(batch) * one_block,
        )

    batches = [[0]] + [[2 * s - 1, 2 * s] for s in range(1, middle)] + [[chips - 1]]
    parts = []
    pins = ()
    for step in range(2, middle + 1):
        incoming = key_ring.front[0]
        key_ring.hop(0, *pins)
        if step == 2:
            parts.append(partners_of(batches[0]))
            pins = (parts[-1][1],)
        if step < middle:
            key_ring.hop(1, *pins)
            parts.append(partners_of(batches[step - 1], *pins))
            pins = (parts[-1][1],)
    query_ring.hop(0, incoming)
    parts.append(partners_of(batches[middle - 1], *pins))
    query_ring.hop(1, parts[-1][1])
    group_total, diag = call(
        functools.partial(group_forward_kernel, loop),
        [shape((1, anchors))] * 2,
        [key_rows] + others + [after(query_rows, parts[-1][1])],
        loop * one_block,
    )
    parts.append(partners_of(batches[middle], group_total))
    logits, payload = call(
        totals_kernel,
        [shape((chips, 2 * anchors)), shape((2 * chips + 1, anchors))],
        [part[1] for part in parts] + [group_total],
        1e6,
    )
    other = swap(payload)
    loss, log_total, home, message, columns, sib_columns = call(
        weights_kernel,
        [
            shape((1, anchors)),
            shape((1, anchors)),
            shape((8, anchors)),
            shape((middle, 8, anchors)),
            shape((anchors, chips + 8)),
            shape((anchors, chips)),
        ],
        [logits, other, codes, sib_codes, group_total, diag],
        1e6,
    )
    arrived = []
    for step in range(middle):
        message = lax.ppermute(message, "sky", onward)
        arrived.append(message[0])
        message = message[1:]

    def grad_keys_of(steps, sums, *pins):
        blocks, sources, messages = [], [], []
        for step in steps:
            slots = [0] if step == 0 else [chips - 1] if step == middle else [2 * step - 1, 2 * step]
            for half, slot in enumerate(slots):
                blocks.append(query_ring.blocks[slot])
                sources.append((len(messages), 4 * half))
            messages.append(arrived[step - 1] if step else home)
        return call(
            functools.partial(grad_key_kernel, sources, len(blocks), len(sums)),
            [shape((anchors, width))] * 2,
            blocks + messages + [after(sums[0], *pins)] + list(sums[1:]),
            2 * len(blocks) * one_block,
        )

    query_ring.hop(0, log_total)
    all_logs = [log_total] + group(log_total)
    (sib_summed_q,) = call(
        functools.partial(grad_sibling_kernel, batches),
        [shape((anchors, width))],
        [part[0] for part in parts] + [sib_columns],
        1e6,
    )
    query_ring.hop(1, sib_summed_q)
    for step in range(3, middle):
        if step < middle - 1:
            query_ring.hop(0)
            query_ring.hop(1)
    (summed_q,) = call(
        functools.partial(grad_query_kernel, batches, loop),
        [shape((anchors, width))],
        [part[0] for part in parts]
        + [key_rows]
        + others
        + [after(query_rows, sib_summed_q), columns],
        2 * loop * one_block,
    )
    query_ring.hop(0, summed_q)
    (group_k,) = call(
        functools.partial(group_key_kernel, loop),
        [shape((anchors, width))],
        [query_rows] + others + all_logs + [after(key_rows, summed_q), inverse],
        2 * loop * one_block,
    )
    query_ring.hop(1, group_k)
    summed_k = grad_keys_of([0, 1], [group_k])
    query_ring.hop(0, summed_k[0])
    (grad_queries,) = call(
        finish_kernel,
        [shape((anchors, width))],
        [queries, after(summed_q, summed_k[0]), swap(sib_summed_q)],
        1e6,
    )
    for step in range(2, middle + 1):
        summed_k = grad_keys_of([step], summed_k)
    (grad_keys,) = call(
        finish_kernel,
        [shape((anchors, width))],
        [keys, summed_k[0], swap(summed_k[1])],
        1e6,
    )
    return (loss.reshape(anchors), grad_queries, grad_keys)


def solution(mesh):
    in_specs = (
        P(("sky", "loop"), None),
        P(("sky", "loop"), None),
        P(("sky", "loop"), None),
        P(("sky", "loop"), None),
        P(("sky", "loop")),
    )
    out_specs = (P(("sky", "loop")), P(("sky", "loop"), None), P(("sky", "loop"), None))
    return jax.shard_map(shards, mesh=mesh, in_specs=in_specs, out_specs=out_specs, check_vma=False)
```

```python
import functools

import jax
import jax.numpy as jnp
import numpy as np
from jax import lax
from jax.experimental import pallas as pl
from jax.experimental.pallas import tpu as pltpu
from jax.sharding import PartitionSpec as P

SCALE = 10.0
EPS = 1e-06
F32 = jnp.float32
BF16 = jnp.bfloat16
CODE_BASE = 32.0
HEAVY = 3e9
SPARE_BYTES = 6 * 1024 * 1024


def chip_ring(chips):
    width = 2 if chips <= 8 else 4
    if chips % width or (chips // width) % 2:
        return list(range(chips))
    height = chips // width
    order = []
    for row in range(height):
        columns = range(1, width) if row % 2 == 0 else range(width - 1, 0, -1)
        order += [row * width + column for column in columns]
    order += [row * width for row in range(height - 1, -1, -1)]
    return order


def padded(x):
    dims = (1, 1) + tuple(x.shape)
    size = jnp.dtype(x.dtype).itemsize
    rows = 32 // size
    tile = -(-dims[-2] // rows) * rows * -(-dims[-1] // 128) * 128
    return int(np.prod(dims[:-2])) * tile * size


def call(kernel, outs, operands, flops, smem=()):
    moved = sum(padded(x) for x in list(operands) + list(outs))
    specs = [
        pl.BlockSpec(memory_space=pltpu.SMEM if i in smem else pltpu.VMEM)
        for i in range(len(operands))
    ]
    return pl.pallas_call(
        kernel,
        out_shape=list(outs),
        in_specs=specs,
        out_specs=[pl.BlockSpec(memory_space=pltpu.VMEM)] * len(outs),
        compiler_params=pltpu.CompilerParams(vmem_limit_bytes=moved + SPARE_BYTES),
        cost_estimate=pl.CostEstimate(flops=int(flops), bytes_accessed=moved, transcendentals=0),
    )(*operands)


def shape(dims, dtype=F32):
    return jax.ShapeDtypeStruct(dims, dtype)


def message_rows(middle):
    return -(-(12 * (middle - 1) + 6) // 16) * 16


def unit_of(rows):
    wide = rows.astype(F32)
    norms = jnp.sqrt(jnp.sum(wide * wide, axis=1, keepdims=True) + EPS)
    return wide / norms, norms


def back_unit(unit, norms, grad):
    return (grad - unit * jnp.sum(unit * grad, axis=1, keepdims=True)) / norms


def dot_t(a, b):
    return lax.dot_general(a, b, (((1,), (1,)), ((), ())), preferred_element_type=F32)


def dot(a, b):
    return jnp.dot(a, b, preferred_element_type=F32)


def row_ids(rows, columns, offset=0):
    return (lax.broadcasted_iota(jnp.int32, (rows, columns), 0) + offset).astype(F32)


def column_ids(rows, columns, offset=0):
    return (lax.broadcasted_iota(jnp.int32, (rows, columns), 1) + offset).astype(F32)


def unit_kernel(x_ref, unit_ref):
    unit_ref[...] = unit_of(x_ref[...])[0].astype(BF16)


def codes_kernel(
    table_ref, owner_ref, row_ref, count_ref, codes_ref, inverse_ref, columns_ref
):
    slots = owner_ref.shape[0]
    places = codes_ref.shape[0] - 1
    count = count_ref[...].reshape(1, count_ref.shape[0])
    inverse = 1.0 / (1.0 + count.astype(F32))
    inverse_ref[...] = inverse
    codes_ref[places : places + 1, :] = inverse
    me = lax.axis_index("sky")
    for place in range(places):
        owner = table_ref[me, place]
        code = jnp.full(count.shape, -1, jnp.int32)
        for slot in range(slots):
            here = (owner_ref[slot : slot + 1, :] == owner) & (slot < count)
            code = jnp.where(here, row_ref[slot : slot + 1, :], code)
        codes_ref[place : place + 1, :] = code.astype(F32)
    columns_ref[...] = codes_ref[...].T


def group_forward_kernel(groups, k_ref, *refs):
    others = refs[: groups - 1]
    q_ref, total_ref, diag_ref = refs[groups - 1 :]
    anchors = q_ref.shape[0]
    step = 256
    for start in range(0, anchors, step):
        q = q_ref[start : start + step, :]
        total = jnp.zeros((1, step), F32)
        for index in range(groups):
            keys = others[index - 1][...] if index else k_ref[...]
            scores = SCALE * dot_t(keys, q)
            total += jnp.sum(jnp.exp(scores), axis=0, keepdims=True)
            if index == 0:
                same = row_ids(anchors, step) == column_ids(anchors, step, start)
                diag = jnp.sum(jnp.where(same, scores, 0.0), axis=0, keepdims=True)
        total_ref[:, start : start + step] = total
        diag_ref[:, start : start + step] = diag


def turn_kernel(rows_ref, columns_ref):
    columns_ref[...] = rows_ref[...].T


def partner_kernel(places, *refs):
    blocks = refs[: len(places)]
    q_ref, s_ref, own_ref, sib_ref, keys_ref, logits_ref = refs[len(places) :]
    anchors = q_ref.shape[0]
    step = 256
    chips = own_ref.shape[1] // 2
    for side, (rows_ref, code_ref) in enumerate(((q_ref, own_ref), (s_ref, sib_ref))):
        for start in range(0, anchors, step):
            rows = slice(start, start + step)
            here = slice(side * anchors + start, side * anchors + start + step)
            q = rows_ref[rows, :].astype(F32)
            logits = []
            for slot, (place, block) in enumerate(zip(places, blocks)):
                at = side * chips + place
                code = code_ref[rows, at : at + 1]
                hot = jnp.where(code == column_ids(step, anchors), 1.0, 0.0).astype(BF16)
                named = dot(hot, block[...])
                keys_ref[slot, here, :] = named.astype(BF16)
                logits.append(SCALE * jnp.sum(named * q, axis=1, keepdims=True))
            logits_ref[here, :] = jnp.concatenate(logits, axis=1)


def totals_kernel(*refs):
    parts = refs[:-3]
    group_ref, logits_ref, payload_ref = refs[-3:]
    anchors = group_ref.shape[1]
    turned = jnp.concatenate([part[...] for part in parts], axis=1).T
    chips = turned.shape[0]
    logits_ref[...] = turned
    payload_ref[:chips, :] = turned[:, anchors:]
    payload_ref[chips : 2 * chips, :] = turned[:, :anchors]
    payload_ref[2 * chips :, :] = group_ref[...]


def weights_kernel(
    logits_ref,
    other_ref,
    own_ref,
    sib_ref,
    group_ref,
    diag_ref,
    loss_ref,
    log_ref,
    home_ref,
    message_ref,
    columns_ref,
    sib_columns_ref,
):
    chips, anchors = logits_ref.shape[0], group_ref.shape[1]

    def all_weights(near, far, near_codes, far_codes, group, inverse):
        total, chosen = group, jnp.zeros((1, anchors), F32)
        for logits, codes in ((near, near_codes), (far, far_codes)):
            live = codes >= 0
            total += jnp.sum(jnp.where(live, jnp.exp(logits), 0.0), axis=0, keepdims=True)
            chosen += jnp.sum(jnp.where(live, logits, 0.0), axis=0, keepdims=True)
        log_total = jnp.log(total)
        near, far = (
            jnp.where(codes >= 0, jnp.exp(logits - log_total) - inverse, 0.0)
            for logits, codes in ((near, near_codes), (far, far_codes))
        )
        return log_total, chosen, near, far

    inverse = own_ref[2 * chips :, :]
    near_code, far_code = own_ref[:chips, :], own_ref[chips : 2 * chips, :]
    sib_near_code, sib_far_code = sib_ref[chips : 2 * chips, :], sib_ref[:chips, :]
    log_total, chosen, near, far = all_weights(
        logits_ref[:, :anchors],
        other_ref[:chips, :],
        near_code,
        far_code,
        group_ref[...],
        inverse,
    )
    loss_ref[...] = log_total - inverse * (diag_ref[...] + chosen)
    log_ref[...] = log_total
    unused, unused, sib_near, sib_far = all_weights(
        logits_ref[:, anchors:],
        other_ref[chips : 2 * chips, :],
        sib_near_code,
        sib_far_code,
        other_ref[2 * chips :, :],
        sib_ref[2 * chips :, :],
    )
    filler = jnp.zeros((6, anchors), F32)
    columns_ref[...] = jnp.concatenate([near, log_total, inverse, filler], axis=0).T
    sib_columns_ref[...] = sib_near.T

    def row(x, slot):
        return x[slot : slot + 1, :]

    def both_sides(slot):
        return [row(near_code, slot), row(far_code, slot), row(near, slot), row(far, slot)]

    home_ref[...] = jnp.concatenate(both_sides(0), axis=0)
    def coded(codes, weights):
        high = [jnp.floor(code / CODE_BASE) for code in codes]
        return high + [code - CODE_BASE * h for code, h in zip(codes, high)] + weights

    rows = []
    for slot in range(2, chips - 1, 2):
        for codes, weights in ((far_code, far), (sib_far_code, sib_far)):
            pair = (slot, slot - 1)
            rows += coded([row(codes, at) for at in pair], [row(weights, at) for at in pair])
    codes = [row(near_code, chips - 1), row(sib_near_code, chips - 1)]
    rows += coded(codes, [row(near, chips - 1), row(sib_near, chips - 1)])
    number = message_rows(chips // 2)
    rows.append(jnp.zeros((number - len(rows), anchors), F32))
    block = jnp.concatenate(rows, axis=0).astype(BF16)
    width = message_ref.shape[1]
    for index in range(anchors // width):
        part = block[:, index * width : (index + 1) * width]
        message_ref[index * number : (index + 1) * number, :] = part


def carrier_kernel(block_ref, message_ref, out_ref):
    rows = block_ref.shape[0]
    out_ref[:rows, :] = block_ref[...]
    out_ref[rows:, :] = message_ref[...]


def partner_sum(columns, order, named, rows):
    total = None
    for place, (ref, slot) in zip(order, named):
        weight = columns[:, place : place + 1].astype(BF16).astype(F32)
        term = weight * ref[slot, rows, :].astype(F32)
        total = term if total is None else total + term
    return total


def named_rows(batches, refs):
    named = [(ref, slot) for ref, places in zip(refs, batches) for slot in range(len(places))]
    return [place for places in batches for place in places], named


def grad_sibling_kernel(batches, *refs):
    order, named = named_rows(batches, refs)
    columns_ref, out_ref = refs[len(batches) :]
    anchors = out_ref.shape[0]
    step = 256
    for start in range(0, anchors, step):
        rows = slice(start, start + step)
        far = slice(anchors + start, anchors + start + step)
        out_ref[rows, :] = partner_sum(columns_ref[rows, :], order, named, far)


def grad_query_kernel(batches, groups, *refs):
    order, named = named_rows(batches, refs)
    rest = refs[len(batches) :]
    k_ref, rest = rest[0], rest[1:]
    others, rest = rest[: groups - 1], rest[groups - 1 :]
    q_ref, columns_ref, out_ref = rest
    anchors = q_ref.shape[0]
    chips = len(order)
    step = 256
    for start in range(0, anchors, step):
        rows = slice(start, start + step)
        columns = columns_ref[rows, :]
        total = partner_sum(columns, order, named, rows)
        q = q_ref[rows, :]
        log_total = columns[:, chips : chips + 1]
        inverse = columns[:, chips + 1 : chips + 2]
        for index in range(groups):
            keys = others[index - 1][...] if index else k_ref[...]
            scores = SCALE * dot_t(q, keys)
            weights = jnp.exp(scores - log_total)
            if index == 0:
                same = row_ids(step, anchors, start) == column_ids(step, anchors)
                weights -= jnp.where(same, inverse, 0.0)
            total += dot(weights.astype(BF16), keys)
        out_ref[rows, :] = total


def grad_query_finish_kernel(x_ref, own_ref, other_ref, row_ref, out_ref, loss_ref):
    unit, norms = unit_of(x_ref[...])
    out_ref[...] = back_unit(unit, norms, SCALE * (own_ref[...] + other_ref[...]))
    loss_ref[...] = row_ref[...].reshape(loss_ref.shape[0])


def group_key_kernel(groups, *refs):
    q_ref, others, logs = refs[0], refs[1:groups], refs[groups : 2 * groups]
    k_ref, inv_ref, out_ref = refs[2 * groups :]
    anchors, width = k_ref.shape
    step = 256
    for start in range(0, anchors, step):
        rows = slice(start, start + step)
        total = jnp.zeros((step, width), F32)
        for index in range(groups):
            q = others[index - 1][...] if index else q_ref[...]
            scores = SCALE * dot_t(k_ref[rows, :], q)
            weights = jnp.exp(scores - logs[index][...])
            if index == 0:
                same = row_ids(step, anchors, start) == column_ids(step, anchors)
                weights -= jnp.where(same, inv_ref[...], 0.0)
            total += dot(weights.astype(BF16), q)
        out_ref[rows, :] = total


def grad_key_finish_kernel(
    number,
    first,
    x_ref,
    group_ref,
    own_ref,
    other_ref,
    near_ref,
    far_ref,
    message_ref,
    out_ref,
):
    anchors, width = out_ref.shape
    step = 256
    told = read_message(message_ref, 0, number, first, anchors)
    for start in range(0, anchors, step):
        rows = slice(start, start + step)
        total = group_ref[rows, :] + own_ref[rows, :] + other_ref[rows, :]
        for side, block in enumerate((near_ref, far_ref)):
            code = told[side : side + 1, :]
            weight = told[2 + side : 3 + side, :]
            spread = jnp.where(row_ids(step, anchors, start) == code, weight, 0.0)
            total += dot(spread.astype(BF16), block[:anchors, :])
        unit, norms = unit_of(x_ref[rows, :])
        out_ref[rows, :] = back_unit(unit, norms, SCALE * total)


def read_message(ref, begin, number, first, anchors):
    parts = []
    for index in range(anchors // ref.shape[1]):
        start = begin + index * number
        part = ref[start : start + number, :].astype(F32)[first : first + 6, :]
        parts.append(jnp.concatenate([CODE_BASE * part[:2, :] + part[2:4, :], part[4:6, :]], axis=0))
    return jnp.concatenate(parts, axis=1)


def grad_key_kernel(sources, blocks, carried, number, *refs):
    queries, messages = refs[:blocks], refs[blocks : -2 - carried]
    so_far, outs = refs[len(refs) - 2 - carried : len(refs) - 2], refs[-2:]
    anchors, width = outs[0].shape
    step = 256
    told = [
        read_message(messages[at], anchors, number, 12 * distance - 12 + 6 * half, anchors)
        if distance
        else messages[at][...]
        for at, distance, half in sources
    ]
    for side, out in enumerate(outs):
        for start in range(0, anchors, step):
            rows = slice(start, start + step)
            total = so_far[side][rows, :] if side < carried else jnp.zeros((step, width), F32)
            for message, block in zip(told, queries):
                code = message[side : side + 1, :]
                weight = message[2 + side : 3 + side, :]
                spread = jnp.where(row_ids(step, anchors, start) == code, weight, 0.0)
                total += dot(spread.astype(BF16), block[:anchors, :])
            out[rows, :] = total


def shards(queries, keys, partner_owner, partner_row, partner_count):
    anchors, width = queries.shape
    sky = lax.axis_size("sky")
    loop = lax.axis_size("loop")
    chips = sky // 2
    middle = chips // 2
    order = chip_ring(chips)
    position = {chip: place for place, chip in enumerate(order)}

    def handled(device):
        chip, core = divmod(device, 2)
        way = 1 if core else -1
        along = [order[(position[chip] + way * step) % chips] for step in range(middle + 1)]
        owners = [device]
        for step in range(1, middle):
            owners += [2 * along[step] + core, 2 * along[step] + 1 - core]
        return owners + [2 * along[middle] + core]

    table = np.array([handled(device) + handled(device ^ 1) for device in range(sky)], np.int32)
    siblings = [(i, i ^ 1) for i in range(sky)]
    onward = []
    for place, chip in enumerate(order):
        onward.append((chip * 2, order[(place + 1) % chips] * 2))
        onward.append((chip * 2 + 1, order[place - 1] * 2 + 1))

    def swap(x):
        return lax.ppermute(x, "sky", siblings)

    def after(x, *others):
        return lax.optimization_barrier((x,) + others)[0] if others else x

    class Ring:
        def __init__(self, own, sibling):
            self.front = [own, sibling]
            self.blocks = [own]

        def hop(self, which, *pins):
            self.front[which] = lax.ppermute(after(self.front[which], *pins), "sky", onward)
            self.blocks.append(self.front[which])

    def group(x):
        shifts = [[(i, (i + s) % loop) for i in range(loop)] for s in range(1, loop)]
        return [lax.ppermute(x, "loop", pairs) for pairs in shifts]

    block = shape((anchors, width), BF16)
    one_block = 2 * anchors * anchors * width
    (key_rows,) = call(unit_kernel, [block], [keys], 5 * keys.size)
    key_ring = Ring(key_rows, swap(key_rows))
    key_ring.hop(0)
    (query_rows,) = call(unit_kernel, [block], [queries], 5 * queries.size)
    codes, inverse, code_columns = call(
        codes_kernel,
        [shape((sky + 1, anchors)), shape((1, anchors)), shape((anchors, sky + 1))],
        [jnp.asarray(table), partner_owner.T, partner_row.T, partner_count],
        1e6,
        smem=(0,),
    )
    key_ring.hop(1, codes)
    sib_queries = swap(query_rows)
    query_ring = Ring(query_rows, sib_queries)
    sib_codes = swap(codes)
    (sib_code_columns,) = call(turn_kernel, [shape((anchors, sky + 1))], [sib_codes], 1e6)
    group_keys = group(key_rows)

    def partners_of(batch, *pins):
        return call(
            functools.partial(partner_kernel, batch),
            [shape((len(batch), 2 * anchors, width), BF16), shape((2 * anchors, len(batch)))],
            [key_ring.blocks[place] for place in batch]
            + [after(query_rows, *pins), sib_queries, code_columns, sib_code_columns],
            2 * len(batch) * one_block,
        )

    batches = [[0]] + [[2 * s - 1, 2 * s] for s in range(1, middle)] + [[chips - 1]]
    ring = key_ring.blocks
    key_ring.hop(0)
    parts = [partners_of(batches[0], ring[1])]
    key_ring.hop(1, parts[-1][1])
    parts.append(partners_of(batches[1], parts[-1][1]))
    group_queries = group(after(query_rows, parts[-1][1]))
    for step in range(3, middle + 1):
        key_ring.hop(0, parts[-1][1])
        if step < middle:
            parts.append(partners_of(batches[step - 1], parts[-1][1], ring[2 * step - 2]))
            key_ring.hop(1, parts[-1][1])
    group_total, diag = call(
        functools.partial(group_forward_kernel, loop),
        [shape((1, anchors))] * 2,
        [key_rows] + group_keys + [after(query_rows, parts[-1][1], ring[chips - 3])],
        loop * one_block,
    )
    query_ring.hop(0, group_total)
    parts.append(partners_of(batches[middle - 1], group_total))
    query_ring.hop(1, parts[-1][1])
    parts.append(partners_of(batches[middle], parts[-1][1]))
    logits, payload = call(
        totals_kernel,
        [shape((chips, 2 * anchors)), shape((2 * chips + 1, anchors))],
        [part[1] for part in parts] + [group_total],
        1e6,
    )
    other = swap(payload)
    ring = query_ring.blocks
    each = message_rows(middle)
    rows = each * (anchors // width)
    loss, log_total, home, message, columns, sib_columns = call(
        weights_kernel,
        [
            shape((1, anchors)),
            shape((1, anchors)),
            shape((4, anchors)),
            shape((rows, width), BF16),
            shape((anchors, chips + 8)),
            shape((anchors, chips)),
        ],
        [logits, other, codes, sib_codes, group_total, diag],
        1e6,
    )
    (query_ring.front[0],) = call(
        carrier_kernel, [shape((anchors + rows, width), BF16)], [after(ring[1]), message], 1e6
    )
    query_ring.hop(0)

    def grad_keys_of(steps, sums, *pins):
        blocks, sources, messages = [], [], []
        for step in steps:
            for half, slot in enumerate([2 * step - 1, 2 * step] if step else [0]):
                blocks.append(ring[slot])
                sources.append((len(messages), step, half))
            messages.append(ring[min(2 * step + 1, chips - 1)] if step else home)
        blocks[0] = after(blocks[0], *pins)
        return call(
            functools.partial(grad_key_kernel, sources, len(blocks), len(sums), each),
            [shape((anchors, width))] * 2,
            blocks + messages + list(sums),
            2 * len(blocks) * one_block,
        )

    all_logs = [log_total] + group(log_total)
    (sib_summed_q,) = call(
        functools.partial(grad_sibling_kernel, batches),
        [shape((anchors, width))],
        [part[0] for part in parts] + [after(sib_columns, ring[2])],
        HEAVY,
    )
    query_ring.hop(1, sib_summed_q)
    for step in range(3, middle):
        if step < middle - 1:
            query_ring.hop(0)
            query_ring.hop(1)
    (summed_q,) = call(
        functools.partial(grad_query_kernel, batches, loop),
        [shape((anchors, width))],
        [part[0] for part in parts]
        + [key_rows]
        + group_keys
        + [after(query_rows, sib_summed_q), columns],
        2 * loop * one_block,
    )
    query_ring.hop(0, summed_q)
    summed_k = grad_keys_of([0, 1], [], summed_q)
    query_ring.hop(1)
    (group_k,) = call(
        functools.partial(group_key_kernel, loop),
        [shape((anchors, width))],
        [query_rows] + group_queries + all_logs + [after(key_rows, summed_k[0]), inverse],
        2 * loop * one_block,
    )
    query_ring.hop(0)
    for step in range(2, middle - 1):
        summed_k = grad_keys_of([step], summed_k, group_k)
    (grad_queries, loss) = call(
        grad_query_finish_kernel,
        [shape((anchors, width)), shape((anchors,))],
        [queries, after(summed_q, summed_k[0]), swap(sib_summed_q), loss],
        1e6,
    )
    first = 12 * (middle - 1)
    skip = first // 16 * 16
    opposite = ring[-1][anchors:].reshape(anchors // width, each, width)[:, skip:]
    opposite = lax.ppermute(opposite.reshape(-1, width), "sky", onward)
    facing = swap(ring[-1])
    summed_k = grad_keys_of([middle - 1], summed_k, grad_queries, opposite)
    (grad_keys,) = call(
        functools.partial(grad_key_finish_kernel, each - skip, first - skip),
        [shape((anchors, width))],
        [keys, group_k, summed_k[0], swap(summed_k[1]), ring[-1], facing]
        + [opposite],
        2 * one_block,
    )
    return (loss, grad_queries, grad_keys)


def solution(mesh):
    in_specs = (
        P(("sky", "loop"), None),
        P(("sky", "loop"), None),
        P(("sky", "loop"), None),
        P(("sky", "loop"), None),
        P(("sky", "loop")),
    )
    out_specs = (P(("sky", "loop")), P(("sky", "loop"), None), P(("sky", "loop"), None))
    return jax.shard_map(shards, mesh=mesh, in_specs=in_specs, out_specs=out_specs, check_vma=False)
```

```python
import functools

import jax
import jax.numpy as jnp
import numpy as np
from jax import lax
from jax.experimental import pallas as pl
from jax.experimental.pallas import tpu as pltpu
from jax.sharding import PartitionSpec as P

SCALE = 10.0
EPS = 1e-06
F32 = jnp.float32
BF16 = jnp.bfloat16
CODE_BASE = 32.0
HEAVY = 3e9
SPARE_BYTES = 6 * 1024 * 1024


def chip_ring(chips):
    width = 2 if chips <= 8 else 4
    if chips % width or (chips // width) % 2:
        return list(range(chips))
    height = chips // width
    order = []
    for row in range(height):
        columns = range(1, width) if row % 2 == 0 else range(width - 1, 0, -1)
        order += [row * width + column for column in columns]
    order += [row * width for row in range(height - 1, -1, -1)]
    return order


def padded(x):
    dims = (1, 1) + tuple(x.shape)
    size = jnp.dtype(x.dtype).itemsize
    rows = 32 // size
    tile = -(-dims[-2] // rows) * rows * -(-dims[-1] // 128) * 128
    return int(np.prod(dims[:-2])) * tile * size


def call(kernel, outs, operands, flops, smem=()):
    moved = sum(padded(x) for x in list(operands) + list(outs))
    specs = [
        pl.BlockSpec(memory_space=pltpu.SMEM if i in smem else pltpu.VMEM)
        for i in range(len(operands))
    ]
    return pl.pallas_call(
        kernel,
        out_shape=list(outs),
        in_specs=specs,
        out_specs=[pl.BlockSpec(memory_space=pltpu.VMEM)] * len(outs),
        compiler_params=pltpu.CompilerParams(vmem_limit_bytes=moved + SPARE_BYTES),
        cost_estimate=pl.CostEstimate(flops=int(flops), bytes_accessed=moved, transcendentals=0),
    )(*operands)


def shape(dims, dtype=F32):
    return jax.ShapeDtypeStruct(dims, dtype)


def message_rows(middle):
    return -(-(12 * (middle - 1) + 6) // 16) * 16


def unit_of(rows):
    wide = rows.astype(F32)
    norms = jnp.sqrt(jnp.sum(wide * wide, axis=1, keepdims=True) + EPS)
    return wide / norms, norms


def back_unit(unit, norms, grad):
    return (grad - unit * jnp.sum(unit * grad, axis=1, keepdims=True)) / norms


def dot_t(a, b):
    return lax.dot_general(a, b, (((1,), (1,)), ((), ())), preferred_element_type=F32)


def dot(a, b):
    return jnp.dot(a, b, preferred_element_type=F32)


def row_ids(rows, columns, offset=0):
    return (lax.broadcasted_iota(jnp.int32, (rows, columns), 0) + offset).astype(F32)


def column_ids(rows, columns, offset=0):
    return (lax.broadcasted_iota(jnp.int32, (rows, columns), 1) + offset).astype(F32)


def unit_kernel(x_ref, unit_ref):
    unit_ref[...] = unit_of(x_ref[...])[0].astype(BF16)


def codes_kernel(
    table_ref, owner_ref, row_ref, count_ref, codes_ref, inverse_ref, columns_ref
):
    slots = owner_ref.shape[0]
    places = codes_ref.shape[0] - 1
    count = count_ref[...].reshape(1, count_ref.shape[0])
    inverse = 1.0 / (1.0 + count.astype(F32))
    inverse_ref[...] = inverse
    codes_ref[places : places + 1, :] = inverse
    me = lax.axis_index("sky")
    for place in range(places):
        owner = table_ref[me, place]
        code = jnp.full(count.shape, -1, jnp.int32)
        for slot in range(slots):
            here = (owner_ref[slot : slot + 1, :] == owner) & (slot < count)
            code = jnp.where(here, row_ref[slot : slot + 1, :], code)
        codes_ref[place : place + 1, :] = code.astype(F32)
    columns_ref[...] = codes_ref[...].T


def group_forward_kernel(groups, k_ref, *refs):
    others = refs[: groups - 1]
    q_ref, total_ref, diag_ref = refs[groups - 1 :]
    anchors = q_ref.shape[0]
    step = 256
    for start in range(0, anchors, step):
        q = q_ref[start : start + step, :]
        total = jnp.zeros((1, step), F32)
        for index in range(groups):
            keys = others[index - 1][...] if index else k_ref[...]
            scores = SCALE * dot_t(keys, q)
            total += jnp.sum(jnp.exp(scores), axis=0, keepdims=True)
            if index == 0:
                same = row_ids(anchors, step) == column_ids(anchors, step, start)
                diag = jnp.sum(jnp.where(same, scores, 0.0), axis=0, keepdims=True)
        total_ref[:, start : start + step] = total
        diag_ref[:, start : start + step] = diag


def turn_kernel(rows_ref, columns_ref):
    columns_ref[...] = rows_ref[...].T


def partner_kernel(places, *refs):
    blocks = refs[: len(places)]
    q_ref, s_ref, own_ref, sib_ref, keys_ref, logits_ref = refs[len(places) :]
    anchors = q_ref.shape[0]
    step = 256
    chips = own_ref.shape[1] // 2
    for side, (rows_ref, code_ref) in enumerate(((q_ref, own_ref), (s_ref, sib_ref))):
        for start in range(0, anchors, step):
            rows = slice(start, start + step)
            here = slice(side * anchors + start, side * anchors + start + step)
            q = rows_ref[rows, :].astype(F32)
            logits = []
            for slot, (place, block) in enumerate(zip(places, blocks)):
                at = side * chips + place
                code = code_ref[rows, at : at + 1]
                hot = jnp.where(code == column_ids(step, anchors), 1.0, 0.0).astype(BF16)
                named = dot(hot, block[...])
                keys_ref[slot, here, :] = named.astype(BF16)
                logits.append(SCALE * jnp.sum(named * q, axis=1, keepdims=True))
            logits_ref[here, :] = jnp.concatenate(logits, axis=1)


def totals_kernel(*refs):
    parts = refs[:-3]
    group_ref, logits_ref, payload_ref = refs[-3:]
    anchors = group_ref.shape[1]
    turned = jnp.concatenate([part[...] for part in parts], axis=1).T
    chips = turned.shape[0]
    logits_ref[...] = turned
    payload_ref[:chips, :] = turned[:, anchors:]
    payload_ref[chips : 2 * chips, :] = turned[:, :anchors]
    payload_ref[2 * chips :, :] = group_ref[...]


def weights_kernel(
    logits_ref,
    other_ref,
    own_ref,
    sib_ref,
    group_ref,
    diag_ref,
    loss_ref,
    log_ref,
    home_ref,
    message_ref,
    columns_ref,
    sib_columns_ref,
):
    chips, anchors = logits_ref.shape[0], group_ref.shape[1]

    def all_weights(near, far, near_codes, far_codes, group, inverse):
        total, chosen = group, jnp.zeros((1, anchors), F32)
        for logits, codes in ((near, near_codes), (far, far_codes)):
            live = codes >= 0
            total += jnp.sum(jnp.where(live, jnp.exp(logits), 0.0), axis=0, keepdims=True)
            chosen += jnp.sum(jnp.where(live, logits, 0.0), axis=0, keepdims=True)
        log_total = jnp.log(total)
        near, far = (
            jnp.where(codes >= 0, jnp.exp(logits - log_total) - inverse, 0.0)
            for logits, codes in ((near, near_codes), (far, far_codes))
        )
        return log_total, chosen, near, far

    inverse = own_ref[2 * chips :, :]
    near_code, far_code = own_ref[:chips, :], own_ref[chips : 2 * chips, :]
    sib_near_code, sib_far_code = sib_ref[chips : 2 * chips, :], sib_ref[:chips, :]
    log_total, chosen, near, far = all_weights(
        logits_ref[:, :anchors],
        other_ref[:chips, :],
        near_code,
        far_code,
        group_ref[...],
        inverse,
    )
    loss_ref[...] = log_total - inverse * (diag_ref[...] + chosen)
    log_ref[...] = log_total
    unused, unused, sib_near, sib_far = all_weights(
        logits_ref[:, anchors:],
        other_ref[chips : 2 * chips, :],
        sib_near_code,
        sib_far_code,
        other_ref[2 * chips :, :],
        sib_ref[2 * chips :, :],
    )
    filler = jnp.zeros((6, anchors), F32)
    columns_ref[...] = jnp.concatenate([near, log_total, inverse, filler], axis=0).T
    sib_columns_ref[...] = sib_near.T

    def row(x, slot):
        return x[slot : slot + 1, :]

    def both_sides(slot):
        return [row(near_code, slot), row(far_code, slot), row(near, slot), row(far, slot)]

    home_ref[...] = jnp.concatenate(both_sides(0), axis=0)
    def coded(codes, weights):
        high = [jnp.floor(code / CODE_BASE) for code in codes]
        return high + [code - CODE_BASE * h for code, h in zip(codes, high)] + weights

    rows = []
    for slot in range(2, chips - 1, 2):
        for codes, weights in ((far_code, far), (sib_far_code, sib_far)):
            pair = (slot, slot - 1)
            rows += coded([row(codes, at) for at in pair], [row(weights, at) for at in pair])
    codes = [row(near_code, chips - 1), row(sib_near_code, chips - 1)]
    rows += coded(codes, [row(near, chips - 1), row(sib_near, chips - 1)])
    number = message_rows(chips // 2)
    rows.append(jnp.zeros((number - len(rows), anchors), F32))
    block = jnp.concatenate(rows, axis=0).astype(BF16)
    width = message_ref.shape[1]
    for index in range(anchors // width):
        part = block[:, index * width : (index + 1) * width]
        message_ref[index * number : (index + 1) * number, :] = part


def carrier_kernel(block_ref, message_ref, out_ref):
    rows = block_ref.shape[0]
    out_ref[:rows, :] = block_ref[...]
    out_ref[rows:, :] = message_ref[...]


def partner_sum(columns, order, named, rows):
    total = None
    for place, (ref, slot) in zip(order, named):
        weight = columns[:, place : place + 1].astype(BF16).astype(F32)
        term = weight * ref[slot, rows, :].astype(F32)
        total = term if total is None else total + term
    return total


def named_rows(batches, refs):
    named = [(ref, slot) for ref, places in zip(refs, batches) for slot in range(len(places))]
    return [place for places in batches for place in places], named


def grad_sibling_kernel(batches, *refs):
    order, named = named_rows(batches, refs)
    columns_ref, out_ref = refs[len(batches) :]
    anchors = out_ref.shape[0]
    step = 256
    for start in range(0, anchors, step):
        rows = slice(start, start + step)
        far = slice(anchors + start, anchors + start + step)
        out_ref[rows, :] = partner_sum(columns_ref[rows, :], order, named, far)


def grad_query_kernel(batches, groups, *refs):
    order, named = named_rows(batches, refs)
    rest = refs[len(batches) :]
    k_ref, rest = rest[0], rest[1:]
    others, rest = rest[: groups - 1], rest[groups - 1 :]
    q_ref, columns_ref, out_ref = rest
    anchors = q_ref.shape[0]
    chips = len(order)
    step = 256
    for start in range(0, anchors, step):
        rows = slice(start, start + step)
        columns = columns_ref[rows, :]
        total = partner_sum(columns, order, named, rows)
        q = q_ref[rows, :]
        log_total = columns[:, chips : chips + 1]
        inverse = columns[:, chips + 1 : chips + 2]
        for index in range(groups):
            keys = others[index - 1][...] if index else k_ref[...]
            scores = SCALE * dot_t(q, keys)
            weights = jnp.exp(scores - log_total)
            if index == 0:
                same = row_ids(step, anchors, start) == column_ids(step, anchors)
                weights -= jnp.where(same, inverse, 0.0)
            total += dot(weights.astype(BF16), keys)
        out_ref[rows, :] = total


def grad_query_finish_kernel(x_ref, own_ref, other_ref, row_ref, out_ref, loss_ref):
    unit, norms = unit_of(x_ref[...])
    out_ref[...] = back_unit(unit, norms, SCALE * (own_ref[...] + other_ref[...]))
    loss_ref[...] = row_ref[...].reshape(loss_ref.shape[0])


def group_key_kernel(groups, *refs):
    q_ref, others, logs = refs[0], refs[1:groups], refs[groups : 2 * groups]
    k_ref, inv_ref, out_ref = refs[2 * groups :]
    anchors, width = k_ref.shape
    step = 256
    for start in range(0, anchors, step):
        rows = slice(start, start + step)
        total = jnp.zeros((step, width), F32)
        for index in range(groups):
            q = others[index - 1][...] if index else q_ref[...]
            scores = SCALE * dot_t(k_ref[rows, :], q)
            weights = jnp.exp(scores - logs[index][...])
            if index == 0:
                same = row_ids(step, anchors, start) == column_ids(step, anchors)
                weights -= jnp.where(same, inv_ref[...], 0.0)
            total += dot(weights.astype(BF16), q)
        out_ref[rows, :] = total


def grad_key_finish_kernel(
    number,
    first,
    x_ref,
    group_ref,
    own_ref,
    other_ref,
    near_ref,
    far_ref,
    message_ref,
    out_ref,
):
    anchors, width = out_ref.shape
    step = 256
    told = read_message(message_ref, 0, number, first, anchors)
    for start in range(0, anchors, step):
        rows = slice(start, start + step)
        total = group_ref[rows, :] + own_ref[rows, :] + other_ref[rows, :]
        for side, block in enumerate((near_ref, far_ref)):
            code = told[side : side + 1, :]
            weight = told[2 + side : 3 + side, :]
            spread = jnp.where(row_ids(step, anchors, start) == code, weight, 0.0)
            total += dot(spread.astype(BF16), block[:anchors, :])
        unit, norms = unit_of(x_ref[rows, :])
        out_ref[rows, :] = back_unit(unit, norms, SCALE * total)


def read_message(ref, begin, number, first, anchors):
    parts = []
    for index in range(anchors // ref.shape[1]):
        start = begin + index * number
        part = ref[start : start + number, :].astype(F32)[first : first + 6, :]
        parts.append(jnp.concatenate([CODE_BASE * part[:2, :] + part[2:4, :], part[4:6, :]], axis=0))
    return jnp.concatenate(parts, axis=1)


def grad_key_kernel(sources, blocks, carried, number, sides, *refs):
    queries, outs = refs[:blocks], refs[-len(sides) :]
    messages = refs[blocks : -len(sides) - carried]
    so_far = refs[len(refs) - len(sides) - carried : len(refs) - len(sides)]
    anchors, width = outs[0].shape
    step = 256
    told = [
        read_message(messages[at], anchors, number, 12 * distance - 12 + 6 * half, anchors)
        if distance
        else messages[at][...]
        for at, distance, half in sources
    ]
    for index, (side, out) in enumerate(zip(sides, outs)):
        for start in range(0, anchors, step):
            rows = slice(start, start + step)
            total = so_far[index][rows, :] if index < carried else jnp.zeros((step, width), F32)
            for message, block in zip(told, queries):
                code = message[side : side + 1, :]
                weight = message[2 + side : 3 + side, :]
                spread = jnp.where(row_ids(step, anchors, start) == code, weight, 0.0)
                total += dot(spread.astype(BF16), block[:anchors, :])
            out[rows, :] = total


def shards(queries, keys, partner_owner, partner_row, partner_count):
    anchors, width = queries.shape
    sky = lax.axis_size("sky")
    loop = lax.axis_size("loop")
    chips = sky // 2
    middle = chips // 2
    order = chip_ring(chips)
    position = {chip: place for place, chip in enumerate(order)}

    def handled(device):
        chip, core = divmod(device, 2)
        way = 1 if core else -1
        along = [order[(position[chip] + way * step) % chips] for step in range(middle + 1)]
        owners = [device]
        for step in range(1, middle):
            owners += [2 * along[step] + core, 2 * along[step] + 1 - core]
        return owners + [2 * along[middle] + core]

    table = np.array([handled(device) + handled(device ^ 1) for device in range(sky)], np.int32)
    siblings = [(i, i ^ 1) for i in range(sky)]
    onward = []
    for place, chip in enumerate(order):
        onward.append((chip * 2, order[(place + 1) % chips] * 2))
        onward.append((chip * 2 + 1, order[place - 1] * 2 + 1))

    def swap(x):
        return lax.ppermute(x, "sky", siblings)

    def after(x, *others):
        return lax.optimization_barrier((x,) + others)[0] if others else x

    class Ring:
        def __init__(self, own, sibling):
            self.front = [own, sibling]
            self.blocks = [own]

        def hop(self, which, *pins):
            self.front[which] = lax.ppermute(after(self.front[which], *pins), "sky", onward)
            self.blocks.append(self.front[which])

    def group(x):
        shifts = [[(i, (i + s) % loop) for i in range(loop)] for s in range(1, loop)]
        return [lax.ppermute(x, "loop", pairs) for pairs in shifts]

    block = shape((anchors, width), BF16)
    one_block = 2 * anchors * anchors * width
    (key_rows,) = call(unit_kernel, [block], [keys], 5 * keys.size)
    key_ring = Ring(key_rows, None)
    key_ring.hop(0)
    (key_ring.front[1],) = call(unit_kernel, [block], [swap(keys)], 5 * keys.size)
    (query_rows,) = call(unit_kernel, [block], [queries], 5 * queries.size)
    codes, inverse, code_columns = call(
        codes_kernel,
        [shape((sky + 1, anchors)), shape((1, anchors)), shape((anchors, sky + 1))],
        [jnp.asarray(table), partner_owner.T, partner_row.T, partner_count],
        1e6,
        smem=(0,),
    )
    key_ring.hop(1, codes)
    sib_queries = swap(query_rows)
    query_ring = Ring(query_rows, sib_queries)
    sib_codes = swap(codes)
    (sib_code_columns,) = call(turn_kernel, [shape((anchors, sky + 1))], [sib_codes], 1e6)
    group_keys = group(key_rows)

    def partners_of(batch, *pins):
        return call(
            functools.partial(partner_kernel, batch),
            [shape((len(batch), 2 * anchors, width), BF16), shape((2 * anchors, len(batch)))],
            [key_ring.blocks[place] for place in batch]
            + [after(query_rows, *pins), sib_queries, code_columns, sib_code_columns],
            2 * len(batch) * one_block,
        )

    batches = [[0]] + [[2 * s - 1, 2 * s] for s in range(1, middle)] + [[chips - 1]]
    ring = key_ring.blocks
    key_ring.hop(0)
    parts = [partners_of(batches[0], ring[1])]
    key_ring.hop(1, parts[-1][1])
    parts.append(partners_of(batches[1], parts[-1][1]))
    group_queries = group(after(query_rows, parts[-1][1]))
    for step in range(3, middle + 1):
        key_ring.hop(0, parts[-1][1])
        if step < middle:
            parts.append(partners_of(batches[step - 1], parts[-1][1], ring[2 * step - 2]))
            key_ring.hop(1, parts[-1][1])
    group_total, diag = call(
        functools.partial(group_forward_kernel, loop),
        [shape((1, anchors))] * 2,
        [key_rows] + group_keys + [after(query_rows, parts[-1][1], ring[chips - 3])],
        loop * one_block,
    )
    query_ring.hop(0, group_total)
    parts.append(partners_of(batches[middle - 1], group_total))
    query_ring.hop(1, parts[-1][1])
    parts.append(partners_of(batches[middle], parts[-1][1]))
    logits, payload = call(
        totals_kernel,
        [shape((chips, 2 * anchors)), shape((2 * chips + 1, anchors))],
        [part[1] for part in parts] + [group_total],
        1e6,
    )
    other = swap(payload)
    ring = query_ring.blocks
    each = message_rows(middle)
    rows = each * (anchors // width)
    loss, log_total, home, message, columns, sib_columns = call(
        weights_kernel,
        [
            shape((1, anchors)),
            shape((1, anchors)),
            shape((4, anchors)),
            shape((rows, width), BF16),
            shape((anchors, chips + 8)),
            shape((anchors, chips)),
        ],
        [logits, other, codes, sib_codes, group_total, diag],
        1e6,
    )
    (query_ring.front[0],) = call(
        carrier_kernel, [shape((anchors + rows, width), BF16)], [after(ring[1]), message], 1e6
    )
    query_ring.hop(0)

    def grad_keys_of(steps, sums, *pins, sides=(0, 1)):
        blocks, sources, messages = [], [], []
        for step in steps:
            for half, slot in enumerate([2 * step - 1, 2 * step] if step else [0]):
                blocks.append(ring[slot])
                sources.append((len(messages), step, half))
            messages.append(ring[min(2 * step + 1, chips - 1)] if step else home)
        blocks[0] = after(blocks[0], *pins)
        return call(
            functools.partial(grad_key_kernel, sources, len(blocks), len(sums), each, sides),
            [shape((anchors, width))] * len(sides),
            blocks + messages + list(sums),
            2 * len(blocks) * one_block,
        )

    all_logs = [log_total] + group(log_total)
    (sib_summed_q,) = call(
        functools.partial(grad_sibling_kernel, batches),
        [shape((anchors, width))],
        [part[0] for part in parts] + [after(sib_columns, ring[2])],
        HEAVY,
    )
    query_ring.hop(1, sib_summed_q)
    for step in range(3, middle):
        if step < middle - 1:
            query_ring.hop(0)
            query_ring.hop(1)
    (summed_q,) = call(
        functools.partial(grad_query_kernel, batches, loop),
        [shape((anchors, width))],
        [part[0] for part in parts]
        + [key_rows]
        + group_keys
        + [after(query_rows, sib_summed_q), columns],
        2 * loop * one_block,
    )
    query_ring.hop(0, summed_q)
    summed_k = grad_keys_of([0, 1], [], summed_q, *all_logs[1:])
    query_ring.hop(1)
    (group_k,) = call(
        functools.partial(group_key_kernel, loop),
        [shape((anchors, width))],
        [query_rows] + group_queries + all_logs + [after(key_rows, summed_k[0]), inverse],
        2 * loop * one_block,
    )
    query_ring.hop(0, summed_k[0])
    for step in range(2, middle - 1):
        summed_k = grad_keys_of([step], summed_k, group_k)
    (grad_queries, loss) = call(
        grad_query_finish_kernel,
        [shape((anchors, width)), shape((anchors,))],
        [queries, after(summed_q, summed_k[0]), swap(sib_summed_q), loss],
        1e6,
    )
    first = 12 * (middle - 1)
    skip = first // 16 * 16
    opposite = after(ring[-1], grad_queries)[anchors:].reshape(anchors // width, each, width)[:, skip:]
    opposite = lax.ppermute(opposite.reshape(-1, width), "sky", onward)
    facing = swap(ring[-1])
    farthest = [middle - 1]
    (sib_sum,) = grad_keys_of(farthest, summed_k[1:], grad_queries, opposite, sides=(1,))
    (own_sum,) = grad_keys_of(farthest, summed_k[:1], sib_sum, sides=(0,))
    (grad_keys,) = call(
        functools.partial(grad_key_finish_kernel, each - skip, first - skip),
        [shape((anchors, width))],
        [keys, group_k, own_sum, swap(sib_sum), ring[-1], facing, opposite],
        2 * one_block,
    )
    return (loss, grad_queries, grad_keys)


def solution(mesh):
    in_specs = (
        P(("sky", "loop"), None),
        P(("sky", "loop"), None),
        P(("sky", "loop"), None),
        P(("sky", "loop"), None),
        P(("sky", "loop")),
    )
    out_specs = (P(("sky", "loop")), P(("sky", "loop"), None), P(("sky", "loop"), None))
    return jax.shard_map(shards, mesh=mesh, in_specs=in_specs, out_specs=out_specs, check_vma=False)
```
